256 devices in a mesh: batch: 8 (over x, core), slab: 32 (over y, z).
Axes of the slice: x: 4, y: 4, z: 8, core: 2. Of those that a mesh axis runs over, the one named last changes fastest.
Arguments:
- volume: bfloat16 [8, 32, 128, 16, 128], P('batch', None, 'slab'), may hold values from -6 to 6
- kernel: bfloat16 [32, 32, 3, 3, 3], replicated, may hold values from -0.21875 to 0.21875
- offset: float32 [32], replicated, may hold values from -1 to 1
- upstream: bfloat16 [8, 32, 128, 16, 128], P('batch', None, 'slab'), may hold values from -6 to 6
Outputs:
- activated: bfloat16 [8, 32, 128, 16, 128], P('batch', None, 'slab')
- grad_volume: bfloat16 [8, 32, 128, 16, 128], P('batch', None, 'slab')
- grad_kernel: float32 [32, 32, 3, 3, 3], replicated
- grad_offset: float32 [32], replicated
The draws below stay inside these ranges and needn't reach their ends.
All inputs are finite; a program needn't handle non-finite values.
Results may differ from the reference program's by a relative error of at most 0.0085.
Values may be sent and summed in bfloat16 or wider, within the bound.
A program may use at most 64 MiB of HBM per device.

```python
import jax
import jax.numpy as jnp
from jax import lax

CH = 32
ROWS = 16
COLS = 128
SAMPLES = 8
DEPTH = 128


def steps_of(own_key, shape, shards, low, largest):
    factor_of, own = 1.0, jax.random.fold_in(own_key, 6)
    for dim, blocks in shards:
        draws = jnp.exp(jax.random.uniform(jax.random.fold_in(own, dim), (blocks,), jnp.float32, low / len(shards), largest / len(shards)))
        factor_of = factor_of * jnp.repeat(draws, shape[dim] // blocks).reshape([-1 if axis == dim else 1 for axis in range(len(shape))])
    return factor_of


def noise(stream_key, shape, scale, bound, cuts=(), dtype=jnp.bfloat16):
    result = scale * jax.random.normal(stream_key, shape, jnp.float32)
    if cuts:
        result = result * steps_of(stream_key, shape, cuts, -0.22, 0.18)
    return jnp.clip(result, -bound, bound).astype(dtype)


def setup_inputs(seed: int = 0) -> dict:
    seeds = jax.random.split(jax.random.key(seed), 5)
    return {
        "volume": noise(seeds[0], (SAMPLES, CH, DEPTH, ROWS, COLS), 1.0, 6.0, ((0, 8), (2, 32))),
        "kernel": noise(seeds[1], (CH, CH, 3, 3, 3), (27 * CH) ** -0.5, 0.21875),
        "offset": jnp.clip(jax.random.uniform(seeds[2], (CH,), jnp.float32, -1.0, 1.0), -1.0, 1.0),
        "upstream": noise(seeds[3], (SAMPLES, CH, DEPTH, ROWS, COLS), 1.0, 6.0, ((0, 8), (2, 32))),
    }


def convolve(field, weights):
    return lax.conv_general_dilated(field, weights, (1, 1, 1), ((1, 1), (1, 1), (1, 1)), dimension_numbers=('NCDHW', 'OIDHW', 'NCDHW'), preferred_element_type=jnp.float32)

def reference(volume, kernel, offset, upstream):
    preact = convolve(volume, kernel) + offset[None, :, None, None, None]
    sig = jax.nn.sigmoid(preact)
    activated = (preact * sig).astype(jnp.bfloat16)
    grad_pre = (upstream.astype(jnp.float32) * sig * (1.0 + preact * (1.0 - sig))).astype(jnp.bfloat16)
    flipped = jnp.transpose(jnp.flip(kernel, (2, 3, 4)), (1, 0, 2, 3, 4))
    grad_volume = convolve(grad_pre, flipped).astype(jnp.bfloat16)
    depth, rows, cols = (volume.shape[2], volume.shape[3], volume.shape[4])
    scale = 1.0 / jnp.sqrt(jnp.float32(volume.shape[0] * depth * rows * cols))
    padded = jnp.pad(volume, ((0, 0), (0, 0), (1, 1), (1, 1), (1, 1))).astype(jnp.float32)
    grad_wide = grad_pre.astype(jnp.float32)
    terms = []
    for first in range(3):
        for second in range(3):
            for third in range(3):
                window = padded[:, :, first:first + depth, second:second + rows, third:third + cols]
                terms.append(jnp.einsum('nodhw,nidhw->oi', grad_wide, window))
    grad_kernel = jnp.stack(terms, axis=2).reshape(kernel.shape) * scale
    grad_offset = lax.optimization_barrier(jnp.sum(grad_wide, axis=(0, 2, 3, 4))) * scale
    return (activated, grad_volume, grad_kernel, grad_offset)
```

```python
import functools

import jax
import jax.numpy as jnp
from jax import lax
from jax.experimental import pallas as pl
from jax.experimental.pallas import tpu as pltpu
from jax.sharding import PartitionSpec as P

MESH = pl.DeviceIdType.MESH
CH = 32
PLANES = 4
ROWS = 16
COLS = 128
BLOCK = 8
WIN = BLOCK + 2
TAPS = 3 * CH
DEEP = 3 * WIN * TAPS
GROUPS = 4
RING = 8


def banded(base, out_ref):
    for row in range(BLOCK):
        move = row * TAPS
        if move == 0:
            block = base
        else:
            block = jnp.concatenate([base[:, DEEP - move :], base[:, : DEEP - move]], axis=1)
        out_ref[row * CH : (row + 1) * CH, :] = block.astype(jnp.bfloat16)


def base_of(pieces):
    gap = jnp.zeros((CH, (WIN - 3) * TAPS), jnp.float32)
    parts = []
    for plane in pieces:
        parts.extend(plane)
        parts.append(gap)
    return jnp.concatenate(parts, axis=1)


def shifted(values, out_ref, slot, row, flip):
    lane = lax.broadcasted_iota(jnp.int32, (CH, COLS), 1)
    left = jnp.where(lane == 0, 0.0, pltpu.roll(values, 1, 1))
    right = jnp.where(lane == COLS - 1, 0.0, pltpu.roll(values, COLS - 1, 1))
    if flip:
        left, right = right, left
    out_ref[slot, row + 1, 0:CH, :] = left.astype(jnp.bfloat16)
    out_ref[slot, row + 1, CH : 2 * CH, :] = values.astype(jnp.bfloat16)
    out_ref[slot, row + 1, 2 * CH : 3 * CH, :] = right.astype(jnp.bfloat16)


def clear_edges(ref):
    zero = jnp.zeros((TAPS, COLS), jnp.bfloat16)
    for slot in range(PLANES + 2):
        ref[slot, 0] = zero
        ref[slot, ROWS + 1] = zero


def window(ref, slot, half):
    return ref[slot, half * BLOCK : half * BLOCK + WIN].reshape(WIN * TAPS, COLS)


def convolve(src_ref, t_ref, pair, out_ref):
    for half in range(ROWS // BLOCK):
        sides = []
        for slot in pair:
            sides.append(
                jnp.concatenate([window(src_ref, slot + s - 1, half) for s in range(3)], axis=0)
            )
        acc = jnp.dot(
            t_ref[...], jnp.concatenate(sides, axis=1), preferred_element_type=jnp.float32
        )
        for row in range(BLOCK):
            for side in range(2):
                out_ref[side, pl.ds(half * BLOCK + row, CH, stride=ROWS), :] = acc[
                    row * CH : (row + 1) * CH, side * COLS : (side + 1) * COLS
                ]


def weight_terms(gs_ref, xs_ref, pair, dacc_ref, first):
    lane = lax.broadcasted_iota(jnp.int32, (TAPS, COLS), 1) // CH
    for s in range(3):
        total = [None] * 3
        for half in range(ROWS // BLOCK):
            lhs = jnp.concatenate([window(gs_ref, slot, half) for slot in pair], axis=1)
            rhs = jnp.concatenate(
                [
                    xs_ref[
                        slot + s - 1, 1 + half * BLOCK : 1 + half * BLOCK + BLOCK, CH : 2 * CH, :
                    ].reshape(BLOCK * CH, COLS)
                    for slot in pair
                ],
                axis=1,
            )
            prod = lax.dot_general(
                lhs, rhs, (((1,), (1,)), ((), ())), preferred_element_type=jnp.float32
            )
            for kh in range(3):
                for quad in range(2):
                    picked = None
                    for block in range(4):
                        row = quad * 4 + block + 2 - kh
                        value = prod[row * TAPS : (row + 1) * TAPS, quad * COLS : (quad + 1) * COLS]
                        picked = value if picked is None else jnp.where(lane == block, value, picked)
                    total[kh] = picked if total[kh] is None else total[kh] + picked
        for kh in range(3):
            at = pl.ds((s * 3 + kh) * TAPS, TAPS)
            if first:
                dacc_ref[at, :] = total[kh]
            else:
                dacc_ref[at, :] += total[kh]


def body(
    comm,
    scale,
    vol,
    w_ref,
    off_ref,
    up,
    act,
    gvol,
    gk_ref,
    go_ref,
    vown,
    vhalo,
    upn,
    actn,
    gvn,
    xf,
    xs,
    gs,
    tf,
    tb,
    pre,
    dacc,
    oacc,
    pay,
    recv1,
    red,
    recv2,
    res,
    local_sem,
    vsend,
    vrecv,
    gsend,
    grecv,
    rsend,
    rrecv,
):
    if comm:
        batch, slab = lax.axis_index("batch"), lax.axis_index("slab")
        y, z = slab // RING, slab % RING
        members = 8 * GROUPS
        mine = batch * GROUPS + y
        above = (slab + 1) % (GROUPS * RING)
        below = (slab + GROUPS * RING - 1) % (GROUPS * RING)

        def group_peer(i):
            other = (mine + i) % members
            return other, (other // GROUPS, (other % GROUPS) * RING + z)

        def ring_peer(i):
            other = (z + i) % RING
            return other, (batch, y * RING + other)

    load_v = pltpu.make_async_copy(vol, vown, local_sem.at[0])
    load_v.start()
    load_u = pltpu.make_async_copy(up, upn, local_sem.at[1])
    load_u.start()

    if comm:
        barrier = pltpu.get_barrier_semaphore()
        for slot in (above, below):
            pl.semaphore_signal(barrier, 1, device_id=(batch, slot), device_id_type=MESH)

        def greet_ring(i, carry):
            pl.semaphore_signal(barrier, 1, device_id=ring_peer(i)[1], device_id_type=MESH)
            return carry

        def greet_group(i, carry):
            pl.semaphore_signal(barrier, 1, device_id=group_peer(i)[1], device_id_type=MESH)
            return carry

        lax.fori_loop(1, RING, greet_ring, 0)
        lax.fori_loop(1, members, greet_group, 0)
        pl.semaphore_wait(barrier, 2 + RING - 1 + members - 1)
        up_copy = pltpu.make_async_remote_copy(
            vol.at[:, PLANES - 1], vhalo.at[0], vsend.at[0], vrecv.at[0], (batch, above), MESH
        )
        down_copy = pltpu.make_async_remote_copy(
            vol.at[:, 0], vhalo.at[1], vsend.at[1], vrecv.at[1], (batch, below), MESH
        )
        up_copy.start()
        down_copy.start()
        has_below = jnp.where(slab == 0, 0.0, 1.0)
        has_above = jnp.where(slab == GROUPS * RING - 1, 0.0, 1.0)

    clear_edges(xs)
    clear_edges(gs)
    taps = w_ref[...].astype(jnp.float32)
    pieces = [
        [
            jnp.concatenate(
                [taps[((s * 3 + u) * 3 + k) * CH : ((s * 3 + u) * 3 + k + 1) * CH] for k in range(3)],
                axis=1,
            )
            for u in range(3)
        ]
        for s in range(3)
    ]
    banded(base_of(pieces), tf)

    def spread_volume(slot, values):
        xf[slot] = values.astype(jnp.float32).reshape(CH * ROWS, COLS)
        for row in range(ROWS):
            shifted(xf[slot, pl.ds(row, CH, stride=ROWS), :], xs, slot, row, False)

    load_v.wait()
    for plane in range(PLANES):
        spread_volume(plane + 1, vown[:, plane])
    load_u.wait()

    def forward(pair, first):
        convolve(xs, tf, pair, pre)
        for side in range(2):
            plane = pair[side] - 1
            for ch in range(CH):
                at = pl.ds(ch * ROWS, ROWS)
                value = pre[side, at, :] + off_ref[ch]
                sig = 0.5 * jnp.tanh(0.5 * value) + 0.5
                actn[ch, plane] = (value * sig).astype(jnp.bfloat16)
                grad = upn[ch, plane].astype(jnp.float32) * sig * (1.0 + value * (1.0 - sig))
                grad = grad.astype(jnp.bfloat16).astype(jnp.float32)
                pre[side, at, :] = grad
                row = jnp.sum(grad, axis=0, keepdims=True)
                if first and side == 0:
                    oacc[ch : ch + 1, :] = row
                else:
                    oacc[ch : ch + 1, :] += row
            for row in range(ROWS):
                shifted(pre[side, pl.ds(row, CH, stride=ROWS), :], gs, plane + 1, row, True)

    forward((2, 3), True)
    weight_terms(gs, xs, (2, 3), dacc, True)

    if comm:
        up_copy.wait_recv()
        down_copy.wait_recv()
        spread_volume(0, vhalo[0].astype(jnp.float32) * has_below)
        spread_volume(PLANES + 1, vhalo[1].astype(jnp.float32) * has_above)
    else:
        xs[0] = jnp.zeros_like(xs[0])
        xs[PLANES + 1] = jnp.zeros_like(xs[0])
        gs[0] = jnp.zeros_like(xs[0])
        gs[PLANES + 1] = jnp.zeros_like(xs[0])

    forward((1, 4), False)
    store_a = pltpu.make_async_copy(actn, act, local_sem.at[2])
    store_a.start()
    if comm:

        def edge(slot):
            return gs.at[slot, 1 : ROWS + 1, CH : 2 * CH, :]

        gup = pltpu.make_async_remote_copy(
            edge(PLANES), edge(0), gsend.at[0], grecv.at[0], (batch, above), MESH
        )
        gdown = pltpu.make_async_remote_copy(
            edge(1), edge(PLANES + 1), gsend.at[1], grecv.at[1], (batch, below), MESH
        )
        gup.start()
        gdown.start()
    weight_terms(gs, xs, (1, 4), dacc, False)

    packed_rows = 27 * CH // 4
    lane = lax.broadcasted_iota(jnp.int32, (packed_rows, COLS), 1) // CH
    folded = dacc[...]
    folded = folded + pltpu.roll(folded, 2 * CH, 1)
    folded = folded + pltpu.roll(folded, CH, 1)
    packed = folded[:packed_rows]
    for block in range(1, 4):
        packed = jnp.where(
            lane == block, folded[block * packed_rows : (block + 1) * packed_rows], packed
        )
    chunks = packed_rows // 8
    pay[:chunks] = packed.reshape(chunks, 8, COLS)
    pay[chunks : chunks + 4] = oacc[...].reshape(4, 8, COLS)
    pay[chunks + 4 :] = jnp.zeros((32 - chunks - 4, 8, COLS), jnp.float32)

    if comm:

        def scatter(i, carry):
            other, peer = group_peer(i)
            pltpu.make_async_remote_copy(
                pay.at[other], recv1.at[mine], rsend.at[0], rrecv.at[0], peer, MESH
            ).start()
            return carry

        lax.fori_loop(1, members, scatter, 0)
        recv1[mine] = pay[mine]

    turned = taps.T
    pieces = [
        [
            turned[:, ((2 - s) * 3 + 2 - u) * TAPS : ((2 - s) * 3 + 2 - u + 1) * TAPS]
            for u in range(3)
        ]
        for s in range(3)
    ]
    banded(base_of(pieces), tb)

    def backward(pair):
        convolve(gs, tb, pair, pre)
        for side in range(2):
            plane = pair[side] - 1
            gvn[:, plane] = pre[side].reshape(CH, ROWS, COLS).astype(jnp.bfloat16)

    backward((2, 3))

    if comm:
        some = pl.ds(0, members - 1)
        pltpu.make_async_copy(pay.at[some], recv1.at[some], rrecv.at[0]).wait()
        red[...] = jnp.sum(recv1[...], axis=0) * scale

        def exchange(i, carry):
            other, peer = ring_peer(i)
            pltpu.make_async_remote_copy(
                red, recv2.at[z], rsend.at[1], rrecv.at[1], peer, MESH
            ).start()
            return carry

        lax.fori_loop(1, RING, exchange, 0)
        recv2[z] = red[...]

        gup.wait()
        gdown.wait()
        for slot, keep in ((0, has_below), (PLANES + 1, has_above)):
            for row in range(ROWS):
                value = gs[slot, row + 1, CH : 2 * CH, :].astype(jnp.float32) * keep
                shifted(value, gs, slot, row, True)

        few = pl.ds(0, RING - 1)
        pltpu.make_async_copy(recv2.at[few], recv2.at[few], rrecv.at[1]).wait()
        res[mine] = jnp.sum(recv2[...], axis=0)

        def gather(i, carry):
            other, peer = group_peer(i)
            pltpu.make_async_remote_copy(
                res.at[mine], res.at[mine], rsend.at[2], rrecv.at[2], peer, MESH
            ).start()
            return carry

        lax.fori_loop(1, members, gather, 0)
    else:
        res[...] = pay[...] * scale

    backward((1, 4))
    store_g = pltpu.make_async_copy(gvn, gvol, local_sem.at[3])
    store_g.start()

    if comm:
        pltpu.make_async_copy(pay.at[some], recv1.at[some], rrecv.at[2]).wait()
    full = res[:chunks].reshape(packed_rows, COLS)
    for block in range(4):
        moved = full if block == 0 else pltpu.roll(full, COLS - block * CH, 1)
        gk_ref[block * packed_rows : (block + 1) * packed_rows, :] = moved[:, :CH]
    biases = res[chunks : chunks + 4].reshape(CH, COLS)
    go_ref[...] = jnp.sum(biases.T, axis=0, keepdims=True)

    store_a.wait()
    store_g.wait()
    if comm:
        up_copy.wait_send()
        down_copy.wait_send()
        pltpu.make_async_copy(pay.at[some], recv1.at[some], rsend.at[0]).wait()
        pltpu.make_async_copy(recv2.at[few], recv2.at[few], rsend.at[1]).wait()
        pltpu.make_async_copy(pay.at[some], recv1.at[some], rsend.at[2]).wait()


def layer(comm, scale, volume, kernel, offset, upstream):
    taps = jnp.transpose(kernel, (2, 3, 4, 0, 1)).reshape(27 * CH, CH)
    shape = (CH, PLANES, ROWS, COLS)
    wide = (PLANES + 2, ROWS + 2, TAPS, COLS)
    half, full = jnp.bfloat16, jnp.float32
    hbm = pl.BlockSpec(memory_space=pl.ANY)
    vmem = pl.BlockSpec(memory_space=pltpu.VMEM)
    act, gvol, gk, go = pl.pallas_call(
        functools.partial(body, comm, scale),
        out_shape=(
            jax.ShapeDtypeStruct(shape, half),
            jax.ShapeDtypeStruct(shape, half),
            jax.ShapeDtypeStruct((27 * CH, CH), full),
            jax.ShapeDtypeStruct((1, CH), full),
        ),
        in_specs=[hbm, vmem, pl.BlockSpec(memory_space=pltpu.SMEM), hbm],
        out_specs=(hbm, hbm, vmem, vmem),
        scratch_shapes=[
            pltpu.VMEM(shape, half),
            pltpu.VMEM((2, CH, ROWS, COLS), half),
            pltpu.VMEM(shape, half),
            pltpu.VMEM(shape, half),
            pltpu.VMEM(shape, half),
            pltpu.VMEM((PLANES + 2, CH * ROWS, COLS), full),
            pltpu.VMEM(wide, half),
            pltpu.VMEM(wide, half),
            pltpu.VMEM((BLOCK * CH, DEEP), half),
            pltpu.VMEM((BLOCK * CH, DEEP), half),
            pltpu.VMEM((2, CH * ROWS, COLS), full),
            pltpu.VMEM((27 * CH, COLS), full),
            pltpu.VMEM((CH, COLS), full),
            pltpu.VMEM((32, 8, COLS), full),
            pltpu.VMEM((32, 8, COLS), full),
            pltpu.VMEM((8, COLS), full),
            pltpu.VMEM((RING, 8, COLS), full),
            pltpu.VMEM((32, 8, COLS), full),
            pltpu.SemaphoreType.DMA((4,)),
            pltpu.SemaphoreType.DMA((2,)),
            pltpu.SemaphoreType.DMA((2,)),
            pltpu.SemaphoreType.DMA((2,)),
            pltpu.SemaphoreType.DMA((2,)),
            pltpu.SemaphoreType.DMA((3,)),
            pltpu.SemaphoreType.DMA((3,)),
        ],
        compiler_params=pltpu.CompilerParams(
            vmem_limit_bytes=48 * 1024 * 1024,
            **({"collective_id": 0, "has_side_effects": True} if comm else {}),
        ),
        cost_estimate=pl.CostEstimate(flops=10**10, bytes_accessed=4 * 10**6, transcendentals=10**6),
    )(volume.reshape(shape), taps, offset, upstream.reshape(shape))
    return (
        act.reshape(volume.shape),
        gvol.reshape(volume.shape),
        jnp.transpose(gk.reshape(3, 3, 3, CH, CH), (3, 4, 0, 1, 2)),
        go.reshape(CH),
    )


def solution(mesh):
    cells = mesh.shape["batch"] * mesh.shape["slab"] * PLANES * ROWS * COLS
    split = P("batch", None, "slab", None, None)
    return jax.shard_map(
        functools.partial(layer, True, cells**-0.5),
        mesh=mesh,
        in_specs=(split, P(), P(), split),
        out_specs=(split, split, P(), P()),
        check_vma=False,
    )
```

```python
import functools

import jax
import jax.numpy as jnp
from jax import lax
from jax.experimental import pallas as pl
from jax.experimental.pallas import tpu as pltpu
from jax.sharding import PartitionSpec as P

MESH = pl.DeviceIdType.MESH
VMEM = 65_500_000
CH = 32
PLANES = 4
ROWS = 16
COLS = 128
BLOCK = 8
WIN = BLOCK + 2
TAPS = 3 * CH
DEEP = WIN * TAPS
GROUPS = 4
RING = 8
MEMBERS = 8 * GROUPS
PACKED = 27 * CH // 4
CHUNKS = PACKED // 8


def banded(pieces, out_ref, plane):
    whole = jnp.concatenate(pieces, axis=1)
    for row in range(BLOCK):
        parts = [whole]
        if row > 0:
            parts.insert(0, jnp.zeros((CH, row * TAPS), jnp.float32))
        if row < BLOCK - 1:
            parts.append(jnp.zeros((CH, (BLOCK - 1 - row) * TAPS), jnp.float32))
        block = jnp.concatenate(parts, axis=1)
        out_ref[plane, row * CH : (row + 1) * CH, :] = block.astype(jnp.bfloat16)


def shifted(values, out_ref, slot, row, flip):
    lane = lax.broadcasted_iota(jnp.int32, (CH, COLS), 1)
    left = jnp.where(lane == 0, 0.0, pltpu.roll(values, 1, 1))
    right = jnp.where(lane == COLS - 1, 0.0, pltpu.roll(values, COLS - 1, 1))
    if flip:
        left, right = right, left
    out_ref[slot, row + 1, 0:CH, :] = left.astype(jnp.bfloat16)
    out_ref[slot, row + 1, CH : 2 * CH, :] = values.astype(jnp.bfloat16)
    out_ref[slot, row + 1, 2 * CH : 3 * CH, :] = right.astype(jnp.bfloat16)


def clear_edges(ref):
    zero = jnp.zeros((TAPS, COLS), jnp.bfloat16)
    for slot in range(PLANES + 2):
        ref[slot, 0] = zero
        ref[slot, ROWS + 1] = zero


def window(ref, slot, half):
    return ref[slot, half * BLOCK : half * BLOCK + WIN].reshape(DEEP, COLS)


def convolve(src_ref, t_ref, terms, sides, out_ref, add):
    for half in range(ROWS // BLOCK):
        acc = None
        for s, slots in terms:
            rhs = jnp.concatenate([window(src_ref, slot, half) for slot in slots], axis=1)
            part = jnp.dot(t_ref[s], rhs, preferred_element_type=jnp.float32)
            acc = part if acc is None else acc + part
        for row in range(BLOCK):
            for place, side in enumerate(sides):
                at = pl.ds(half * BLOCK + row, CH, stride=ROWS)
                value = acc[row * CH : (row + 1) * CH, place * COLS : (place + 1) * COLS]
                if add:
                    value = value + out_ref[side, at, :]
                out_ref[side, at, :] = value


def inner(src_ref, t_ref, out_ref):
    convolve(src_ref, t_ref, [(s, (1 + s, 2 + s)) for s in range(3)], (0, 1), out_ref, False)


def outer_own(src_ref, t_ref, out_ref):
    convolve(src_ref, t_ref, [(1, (1, PLANES))], (0, 1), out_ref, False)
    convolve(src_ref, t_ref, [(2, (2,))], (0,), out_ref, True)
    convolve(src_ref, t_ref, [(0, (PLANES - 1,))], (1,), out_ref, True)


def outer_halo(src_ref, t_ref, out_ref):
    convolve(src_ref, t_ref, [(0, (0,))], (0,), out_ref, True)
    convolve(src_ref, t_ref, [(2, (PLANES + 1,))], (1,), out_ref, True)


def weight_terms(gs_ref, xs_ref, pair, dacc_ref, first):
    lane = lax.broadcasted_iota(jnp.int32, (TAPS, COLS), 1) // CH
    for s in range(3):
        total = [None] * 3
        for half in range(ROWS // BLOCK):
            lhs = jnp.concatenate([window(gs_ref, slot, half) for slot in pair], axis=1)
            rhs = jnp.concatenate(
                [
                    xs_ref[
                        slot + s - 1, 1 + half * BLOCK : 1 + half * BLOCK + BLOCK, CH : 2 * CH, :
                    ].reshape(BLOCK * CH, COLS)
                    for slot in pair
                ],
                axis=1,
            )
            prod = lax.dot_general(
                lhs, rhs, (((1,), (1,)), ((), ())), preferred_element_type=jnp.float32
            )
            for kh in range(3):
                for quad in range(2):
                    picked = None
                    for block in range(4):
                        row = quad * 4 + block + 2 - kh
                        value = prod[row * TAPS : (row + 1) * TAPS, quad * COLS : (quad + 1) * COLS]
                        picked = value if picked is None else jnp.where(lane == block, value, picked)
                    total[kh] = picked if total[kh] is None else total[kh] + picked
        for kh in range(3):
            at = pl.ds((s * 3 + kh) * TAPS, TAPS)
            if first:
                dacc_ref[at, :] = total[kh]
            else:
                dacc_ref[at, :] += total[kh]


class Peers:
    def __init__(self):
        self.batch, self.slab = lax.axis_index("batch"), lax.axis_index("slab")
        self.y, self.z = self.slab // RING, self.slab % RING
        x, core = self.batch // 2, self.batch % 2
        self.mine = self.batch * GROUPS + self.y
        xs = [wrapped(x + d, 4) for d in range(4)]
        cores = [core, 1 - core]
        ys = [wrapped(self.y + d, GROUPS) for d in range(GROUPS)]
        zs = [wrapped(self.z + d, RING) for d in range(RING)]
        group = [(dx, dy, dc) for dx in range(4) for dy in range(GROUPS) for dc in range(2)]
        group = sorted(group[1:], key=lambda t: -(min(t[0], 4 - t[0]) + min(t[1], GROUPS - t[1])))
        self.group = []
        for dx, dy, dc in group:
            batch = xs[dx] * 2 + cores[dc]
            self.group.append((batch * GROUPS + ys[dy], (batch, ys[dy] * RING + self.z)))
        ring = sorted(range(1, RING), key=lambda d: -min(d, RING - d))
        self.ring = [(zs[d], (self.batch, self.y * RING + zs[d])) for d in ring]

        def place(dx=0, dy=0, dz=0, dc=0):
            return (xs[dx] * 2 + cores[dc], ys[dy] * RING + zs[dz])

        self.x_near = [place(dx=1), place(dx=3)]
        self.x_all = [place(dx=1), place(dx=3), place(dx=2)]
        self.y_near = [place(dy=1), place(dy=GROUPS - 1)]
        self.z_near = [place(dz=1), place(dz=RING - 1)]
        self.z_next = [place(dz=2), place(dz=RING - 2)]
        self.twin = place(dc=1)
        self.above = (self.batch, wrapped(self.slab + 1, GROUPS * RING))
        self.below = (self.batch, wrapped(self.slab + GROUPS * RING - 1, GROUPS * RING))


def wrapped(value, count):
    return jnp.where(value >= count, value - count, value)


def remote(src, dst, send, recv, peer):
    return pltpu.make_async_remote_copy(src, dst, send, recv, peer, MESH)


def tell(sem, peers):
    for peer in peers:
        pl.semaphore_signal(sem, 1, device_id=peer, device_id_type=MESH)


def body(
    comm,
    scale,
    vol,
    w_hbm,
    off_hbm,
    up,
    actn,
    gvn,
    res,
    w_ref,
    off_ref,
    vown,
    vhalo,
    upn,
    xf,
    xs,
    gs,
    tf,
    tb,
    pre_in,
    pre_out,
    dacc,
    oacc,
    pay,
    recv1,
    red,
    recv2,
    final,
    local_sem,
    vsend,
    vrecv,
    gsend,
    grecv,
    rsend,
    rrecv,
    known,
):
    if comm:
        peers = Peers()
        group, ring = peers.group, peers.ring
        barrier = pltpu.get_barrier_semaphore()
        near = [peers.above, peers.below] + peers.z_near + peers.y_near + peers.x_near
        near.append(peers.twin)
        tell(barrier, near)

    load_w = pltpu.make_async_copy(w_hbm, w_ref, local_sem.at[4])
    load_w.start()
    load_v = pltpu.make_async_copy(vol, vown, local_sem.at[0])
    load_v.start()
    load_o = pltpu.make_async_copy(off_hbm, off_ref, local_sem.at[5])
    load_o.start()
    load_u = pltpu.make_async_copy(up, upn, local_sem.at[1])
    load_u.start()
    clear_edges(xs)
    clear_edges(gs)

    if comm:
        pl.semaphore_wait(barrier, len(near))
        up_copy = remote(vol.at[:, PLANES - 1], vhalo.at[0], vsend.at[0], vrecv.at[0], peers.above)
        down_copy = remote(vol.at[:, 0], vhalo.at[1], vsend.at[1], vrecv.at[1], peers.below)
        up_copy.start()
        down_copy.start()
        tell(known.at[0], peers.y_near)
        tell(known.at[1], peers.x_near)
        tell(known.at[2], peers.z_near)
        has_below = jnp.where(peers.slab == 0, 0.0, 1.0)
        has_above = jnp.where(peers.slab == GROUPS * RING - 1, 0.0, 1.0)

    load_w.wait()
    taps = w_ref[...].astype(jnp.float32)

    def tap(s, u, k):
        at = ((s * 3 + u) * 3 + k) * CH
        return taps[at : at + CH]

    for s in range(3):
        pieces = [jnp.concatenate([tap(s, u, k) for k in range(3)], axis=1) for u in range(3)]
        banded(pieces, tf, s)

    def spread_volume(slot, values):
        xf[slot] = values.astype(jnp.float32).reshape(CH * ROWS, COLS)
        for row in range(ROWS):
            shifted(xf[slot, pl.ds(row, CH, stride=ROWS), :], xs, slot, row, False)

    if comm:
        for i in range(3):
            pl.semaphore_wait(known.at[i], 2)
        tell(known.at[3], peers.x_all)
        tell(known.at[4], peers.z_next)

    load_v.wait()
    for plane in range(PLANES):
        spread_volume(plane + 1, vown[:, plane])
    load_o.wait()
    load_u.wait()

    def activate(pre, slots, first):
        for side in range(2):
            plane = slots[side] - 1
            for ch in range(CH):
                at = pl.ds(ch * ROWS, ROWS)
                value = pre[side, at, :] + off_ref[ch]
                sig = 0.5 * jnp.tanh(0.5 * value) + 0.5
                actn[ch, plane] = (value * sig).astype(jnp.bfloat16)
                grad = upn[ch, plane].astype(jnp.float32) * sig * (1.0 + value * (1.0 - sig))
                grad = grad.astype(jnp.bfloat16).astype(jnp.float32)
                pre[side, at, :] = grad
                row = jnp.sum(grad, axis=0, keepdims=True)
                if first and side == 0:
                    oacc[ch : ch + 1, :] = row
                else:
                    oacc[ch : ch + 1, :] += row
            for row in range(ROWS):
                shifted(pre[side, pl.ds(row, CH, stride=ROWS), :], gs, plane + 1, row, True)

    inner(xs, tf, pre_in)
    activate(pre_in, (2, 3), True)
    if comm:
        pl.semaphore_wait(known.at[3], 3)
        pl.semaphore_wait(known.at[4], 2)
        tell(known.at[5], [peers.twin])
    weight_terms(gs, xs, (2, 3), dacc, True)
    outer_own(xs, tf, pre_out)

    if comm:
        up_copy.wait_recv()
        down_copy.wait_recv()
        spread_volume(0, vhalo[0].astype(jnp.float32) * has_below)
        spread_volume(PLANES + 1, vhalo[1].astype(jnp.float32) * has_above)
    else:
        for ref in (xs, gs):
            for slot in (0, PLANES + 1):
                ref[slot] = jnp.zeros_like(ref[slot])

    outer_halo(xs, tf, pre_out)
    activate(pre_out, (1, 4), False)
    if comm:

        def edge(slot):
            return gs.at[slot, 1 : ROWS + 1, CH : 2 * CH, :]

        gup = remote(edge(PLANES), edge(0), gsend.at[0], grecv.at[0], peers.above)
        gdown = remote(edge(1), edge(PLANES + 1), gsend.at[1], grecv.at[1], peers.below)
        gup.start()
        gdown.start()
    weight_terms(gs, xs, (1, 4), dacc, False)

    lane = lax.broadcasted_iota(jnp.int32, (PACKED, COLS), 1) // CH
    folded = dacc[...]
    folded = folded + pltpu.roll(folded, 2 * CH, 1)
    folded = folded + pltpu.roll(folded, CH, 1)
    packed = folded[:PACKED]
    for block in range(1, 4):
        packed = jnp.where(lane == block, folded[block * PACKED : (block + 1) * PACKED], packed)
    pay[:CHUNKS] = packed.reshape(CHUNKS, 8, COLS)
    pay[CHUNKS : CHUNKS + 4] = oacc[...].reshape(4, 8, COLS)
    pay[CHUNKS + 4 :] = jnp.zeros((MEMBERS - CHUNKS - 4, 8, COLS), jnp.float32)

    if comm:
        pl.semaphore_wait(known.at[5], 1)
        mine = peers.mine
        for other, peer in group:
            remote(pay.at[other], recv1.at[mine], rsend.at[0], rrecv.at[0], peer).start()
        recv1[mine] = pay[mine]

    turned = taps.T
    for s in range(3):
        pieces = []
        for u in range(3):
            at = ((2 - s) * 3 + 2 - u) * TAPS
            pieces.append(turned[:, at : at + TAPS])
        banded(pieces, tb, s)

    def finish(pre, slots):
        for side in range(2):
            gvn[:, slots[side] - 1] = pre[side].reshape(CH, ROWS, COLS).astype(jnp.bfloat16)

    inner(gs, tb, pre_in)

    if comm:
        some, few = pl.ds(0, MEMBERS - 1), pl.ds(0, RING - 1)
        pltpu.make_async_copy(recv1.at[some], recv1.at[some], rrecv.at[0]).wait()
        red[...] = jnp.sum(recv1[...], axis=0) * scale
        for other, peer in ring:
            remote(red, recv2.at[peers.z], rsend.at[1], rrecv.at[1], peer).start()
        recv2[peers.z] = red[...]

        finish(pre_in, (2, 3))
        outer_own(gs, tb, pre_out)
        gup.wait()
        gdown.wait()
        for slot, keep in ((0, has_below), (PLANES + 1, has_above)):
            for row in range(ROWS):
                value = gs[slot, row + 1, CH : 2 * CH, :].astype(jnp.float32) * keep
                shifted(value, gs, slot, row, True)

        pltpu.make_async_copy(recv2.at[few], recv2.at[few], rrecv.at[1]).wait()
        final[...] = jnp.sum(recv2[...], axis=0)
        for other, peer in group:
            remote(final, res.at[mine], rsend.at[2], rrecv.at[2], peer).start()
        res[mine] = final[...]
    else:
        finish(pre_in, (2, 3))
        outer_own(gs, tb, pre_out)
        res[...] = pay[...] * scale

    outer_halo(gs, tb, pre_out)
    finish(pre_out, (1, 4))
    if comm:
        up_copy.wait_send()
        down_copy.wait_send()
        pltpu.make_async_copy(recv1.at[some], recv1.at[some], rsend.at[0]).wait()
        pltpu.make_async_copy(recv2.at[few], recv2.at[few], rsend.at[1]).wait()
        pltpu.make_async_copy(recv1.at[some], recv1.at[some], rsend.at[2]).wait()
        pltpu.make_async_copy(recv1.at[some], recv1.at[some], rrecv.at[2]).wait()


def write_out(act_in, gvol_in, res, act, gvol, gk, go, gk_ref, go_ref, sem):
    pairs = ((act_in, act), (gvol_in, gvol), (gk_ref, gk), (go_ref, go))
    copies = [pltpu.make_async_copy(src, dst, sem.at[i]) for i, (src, dst) in enumerate(pairs)]
    copies[0].start()
    copies[1].start()
    full = res[:CHUNKS].reshape(PACKED, COLS)
    for block in range(4):
        moved = full if block == 0 else pltpu.roll(full, COLS - block * CH, 1)
        gk_ref[block * PACKED : (block + 1) * PACKED, :] = moved[:, :CH]
    copies[2].start()
    biases = res[CHUNKS : CHUNKS + 4].reshape(CH, COLS)
    go_ref[...] = jnp.sum(biases.T, axis=0, keepdims=True)
    copies[3].start()
    for copy in copies:
        copy.wait()


def layer(comm, scale, volume, kernel, offset, upstream):
    taps = jnp.transpose(kernel, (2, 3, 4, 0, 1)).reshape(27 * CH, CH)
    shape = (CH, PLANES, ROWS, COLS)
    wide = (PLANES + 2, ROWS + 2, TAPS, COLS)
    half, full = jnp.bfloat16, jnp.float32
    hbm = pl.BlockSpec(memory_space=pltpu.HBM)
    vmem = pl.BlockSpec(memory_space=pltpu.VMEM)
    act, gvol, res = pl.pallas_call(
        functools.partial(body, comm, scale),
        out_shape=(
            pltpu.VMEM(shape, half),
            pltpu.VMEM(shape, half),
            pltpu.VMEM((MEMBERS, 8, COLS), full),
        ),
        in_specs=[hbm, hbm, hbm, hbm],
        out_specs=(vmem, vmem, vmem),
        scratch_shapes=[
            pltpu.VMEM((27 * CH, CH), half),
            pltpu.SMEM((CH,), full),
            pltpu.VMEM(shape, half),
            pltpu.VMEM((2, CH, ROWS, COLS), half),
            pltpu.VMEM(shape, half),
            pltpu.VMEM((PLANES + 2, CH * ROWS, COLS), full),
            pltpu.VMEM(wide, half),
            pltpu.VMEM(wide, half),
            pltpu.VMEM((3, BLOCK * CH, DEEP), half),
            pltpu.VMEM((3, BLOCK * CH, DEEP), half),
            pltpu.VMEM((2, CH * ROWS, COLS), full),
            pltpu.VMEM((2, CH * ROWS, COLS), full),
            pltpu.VMEM((27 * CH, COLS), full),
            pltpu.VMEM((CH, COLS), full),
            pltpu.VMEM((MEMBERS, 8, COLS), full),
            pltpu.VMEM((MEMBERS, 8, COLS), full),
            pltpu.VMEM((8, COLS), full),
            pltpu.VMEM((RING, 8, COLS), full),
            pltpu.VMEM((8, COLS), full),
            pltpu.SemaphoreType.DMA((7,)),
            pltpu.SemaphoreType.DMA((2,)),
            pltpu.SemaphoreType.DMA((2,)),
            pltpu.SemaphoreType.DMA((2,)),
            pltpu.SemaphoreType.DMA((2,)),
            pltpu.SemaphoreType.DMA((3,)),
            pltpu.SemaphoreType.DMA((3,)),
            pltpu.SemaphoreType.REGULAR((6,)),
        ],
        compiler_params=pltpu.CompilerParams(
            vmem_limit_bytes=VMEM,
            **({"collective_id": 0, "has_side_effects": True} if comm else {}),
        ),
        cost_estimate=pl.CostEstimate(flops=10**10, bytes_accessed=4 * 10**6, transcendentals=10**6),
    )(volume.reshape(shape), taps, offset, upstream.reshape(shape))
    act, gvol, gk, go = pl.pallas_call(
        write_out,
        out_shape=(
            jax.ShapeDtypeStruct(shape, half),
            jax.ShapeDtypeStruct(shape, half),
            jax.ShapeDtypeStruct((27 * CH, CH), full),
            jax.ShapeDtypeStruct((1, CH), full),
        ),
        in_specs=[vmem, vmem, vmem],
        out_specs=(hbm, hbm, hbm, hbm),
        scratch_shapes=[
            pltpu.VMEM((27 * CH, CH), full),
            pltpu.VMEM((1, CH), full),
            pltpu.SemaphoreType.DMA((4,)),
        ],
        compiler_params=pltpu.CompilerParams(vmem_limit_bytes=8 * 1024 * 1024),
        cost_estimate=pl.CostEstimate(flops=10**5, bytes_accessed=3 * 10**6, transcendentals=0),
    )(act, gvol, res)
    return (
        act.reshape(volume.shape),
        gvol.reshape(volume.shape),
        jnp.transpose(gk.reshape(3, 3, 3, CH, CH), (3, 4, 0, 1, 2)),
        go.reshape(CH),
    )


def solution(mesh):
    cells = mesh.shape["batch"] * mesh.shape["slab"] * PLANES * ROWS * COLS
    split = P("batch", None, "slab", None, None)
    return jax.shard_map(
        functools.partial(layer, True, cells**-0.5),
        mesh=mesh,
        in_specs=(split, P(), P(), split),
        out_specs=(split, split, P(), P()),
        check_vma=False,
    )
```

```python
import functools

import jax
import jax.numpy as jnp
from jax import lax
from jax.experimental import pallas as pl
from jax.experimental.pallas import tpu as pltpu
from jax.sharding import PartitionSpec as P

MESH = pl.DeviceIdType.MESH
VMEM = 65_500_000
CH = 32
PLANES = 4
ROWS = 16
COLS = 128
BLOCK = 8
WIN = BLOCK + 2
TAPS = 3 * CH
DEEP = WIN * TAPS
GROUPS = 4
RING = 8
MEMBERS = 8 * GROUPS
PACKED = 27 * CH // 4
CHUNKS = PACKED // 8


def banded(pieces, out_ref, plane):
    whole = jnp.concatenate(pieces, axis=1)
    for row in range(BLOCK):
        parts = [whole]
        if row > 0:
            parts.insert(0, jnp.zeros((CH, row * TAPS), jnp.float32))
        if row < BLOCK - 1:
            parts.append(jnp.zeros((CH, (BLOCK - 1 - row) * TAPS), jnp.float32))
        block = jnp.concatenate(parts, axis=1)
        out_ref[plane, row * CH : (row + 1) * CH, :] = block.astype(jnp.bfloat16)


def shifted(values, out_ref, slot, row, flip):
    lane = lax.broadcasted_iota(jnp.int32, (CH, COLS), 1)
    left = jnp.where(lane == 0, 0.0, pltpu.roll(values, 1, 1))
    right = jnp.where(lane == COLS - 1, 0.0, pltpu.roll(values, COLS - 1, 1))
    if flip:
        left, right = right, left
    out_ref[slot, row + 1, 0:CH, :] = left.astype(jnp.bfloat16)
    out_ref[slot, row + 1, CH : 2 * CH, :] = values.astype(jnp.bfloat16)
    out_ref[slot, row + 1, 2 * CH : 3 * CH, :] = right.astype(jnp.bfloat16)


def clear_edges(ref):
    zero = jnp.zeros((TAPS, COLS), jnp.bfloat16)
    for slot in range(PLANES + 2):
        ref[slot, 0] = zero
        ref[slot, ROWS + 1] = zero


def window(ref, slot, half):
    return ref[slot, half * BLOCK : half * BLOCK + WIN].reshape(DEEP, COLS)


def convolve(src_ref, t_ref, terms, sides, out_ref, add):
    for half in range(ROWS // BLOCK):
        acc = None
        for s, slots in terms:
            rhs = jnp.concatenate([window(src_ref, slot, half) for slot in slots], axis=1)
            part = jnp.dot(t_ref[s], rhs, preferred_element_type=jnp.float32)
            acc = part if acc is None else acc + part
        for row in range(BLOCK):
            for place, side in enumerate(sides):
                at = pl.ds(half * BLOCK + row, CH, stride=ROWS)
                value = acc[row * CH : (row + 1) * CH, place * COLS : (place + 1) * COLS]
                if add:
                    value = value + out_ref[side, at, :]
                out_ref[side, at, :] = value


def inner(src_ref, t_ref, out_ref):
    convolve(src_ref, t_ref, [(s, (1 + s, 2 + s)) for s in range(3)], (0, 1), out_ref, False)


def outer_own(src_ref, t_ref, out_ref):
    convolve(src_ref, t_ref, [(1, (1, PLANES))], (0, 1), out_ref, False)
    convolve(src_ref, t_ref, [(2, (2,))], (0,), out_ref, True)
    convolve(src_ref, t_ref, [(0, (PLANES - 1,))], (1,), out_ref, True)


def outer_halo(src_ref, t_ref, out_ref):
    convolve(src_ref, t_ref, [(0, (0,))], (0,), out_ref, True)
    convolve(src_ref, t_ref, [(2, (PLANES + 1,))], (1,), out_ref, True)


def weight_terms(gs_ref, xs_ref, pair, dacc_ref, first):
    lane = lax.broadcasted_iota(jnp.int32, (TAPS, COLS), 1) // CH
    for s in range(3):
        total = [None] * 3
        for half in range(ROWS // BLOCK):
            lhs = jnp.concatenate([window(gs_ref, slot, half) for slot in pair], axis=1)
            rhs = jnp.concatenate(
                [
                    xs_ref[
                        slot + s - 1, 1 + half * BLOCK : 1 + half * BLOCK + BLOCK, CH : 2 * CH, :
                    ].reshape(BLOCK * CH, COLS)
                    for slot in pair
                ],
                axis=1,
            )
            prod = lax.dot_general(
                lhs, rhs, (((1,), (1,)), ((), ())), preferred_element_type=jnp.float32
            )
            for kh in range(3):
                for quad in range(2):
                    picked = None
                    for block in range(4):
                        row = quad * 4 + block + 2 - kh
                        value = prod[row * TAPS : (row + 1) * TAPS, quad * COLS : (quad + 1) * COLS]
                        picked = value if picked is None else jnp.where(lane == block, value, picked)
                    total[kh] = picked if total[kh] is None else total[kh] + picked
        for kh in range(3):
            at = pl.ds((s * 3 + kh) * TAPS, TAPS)
            if first:
                dacc_ref[at, :] = total[kh]
            else:
                dacc_ref[at, :] += total[kh]


class Peers:
    def __init__(self):
        self.batch, self.slab = lax.axis_index("batch"), lax.axis_index("slab")
        self.y, self.z = self.slab // RING, self.slab % RING
        x, core = self.batch // 2, self.batch % 2
        self.mine = self.batch * GROUPS + self.y
        xs = [wrapped(x + d, 4) for d in range(4)]
        cores = [core, 1 - core]
        ys = [wrapped(self.y + d, GROUPS) for d in range(GROUPS)]
        zs = [wrapped(self.z + d, RING) for d in range(RING)]
        group = [(dx, dy, dc) for dx in range(4) for dy in range(GROUPS) for dc in range(2)]
        group = sorted(group[1:], key=lambda t: -(min(t[0], 4 - t[0]) + min(t[1], GROUPS - t[1])))
        self.group = []
        for dx, dy, dc in group:
            batch = xs[dx] * 2 + cores[dc]
            self.group.append((batch * GROUPS + ys[dy], (batch, ys[dy] * RING + self.z)))
        ring = sorted(range(1, RING), key=lambda d: -min(d, RING - d))
        self.ring = [(zs[d], (self.batch, self.y * RING + zs[d])) for d in ring]

        def place(dx=0, dy=0, dz=0, dc=0):
            return (xs[dx] * 2 + cores[dc], ys[dy] * RING + zs[dz])

        self.x_near = [place(dx=1), place(dx=3)]
        self.x_all = [place(dx=1), place(dx=3), place(dx=2)]
        self.y_near = [place(dy=1), place(dy=GROUPS - 1)]
        self.z_near = [place(dz=1), place(dz=RING - 1)]
        self.z_next = [place(dz=2), place(dz=RING - 2)]
        self.twin = place(dc=1)
        self.above = (self.batch, wrapped(self.slab + 1, GROUPS * RING))
        self.below = (self.batch, wrapped(self.slab + GROUPS * RING - 1, GROUPS * RING))


def wrapped(value, count):
    return jnp.where(value >= count, value - count, value)


def remote(src, dst, send, recv, peer):
    return pltpu.make_async_remote_copy(src, dst, send, recv, peer, MESH)


def tell(sem, peers):
    for peer in peers:
        pl.semaphore_signal(sem, 1, device_id=peer, device_id_type=MESH)


def body(
    comm,
    scale,
    vol,
    w_hbm,
    off_hbm,
    up,
    actn,
    gvn,
    res,
    w_ref,
    off_ref,
    vown,
    vhalo,
    upn,
    xf,
    xs,
    gs,
    tf,
    tb,
    pre_in,
    pre_out,
    dacc,
    oacc,
    pay,
    recv1,
    red,
    recv2,
    final,
    local_sem,
    vsend,
    vrecv,
    gsend,
    grecv,
    rsend,
    rrecv,
    known,
):
    if comm:
        peers = Peers()
        group, ring = peers.group, peers.ring
        barrier = pltpu.get_barrier_semaphore()
        near = [peers.above, peers.below] + peers.z_near + peers.y_near + peers.x_near
        near.append(peers.twin)
        tell(barrier, near)

    load_w = pltpu.make_async_copy(w_hbm, w_ref, local_sem.at[4])
    load_w.start()
    load_v = pltpu.make_async_copy(vol, vown, local_sem.at[0])
    load_v.start()
    load_o = pltpu.make_async_copy(off_hbm, off_ref, local_sem.at[5])
    load_o.start()
    load_u = pltpu.make_async_copy(up, upn, local_sem.at[1])
    load_u.start()
    clear_edges(xs)
    clear_edges(gs)

    if comm:
        pl.semaphore_wait(barrier, len(near))
        up_copy = remote(vol.at[:, PLANES - 1], vhalo.at[0], vsend.at[0], vrecv.at[0], peers.above)
        down_copy = remote(vol.at[:, 0], vhalo.at[1], vsend.at[1], vrecv.at[1], peers.below)
        up_copy.start()
        down_copy.start()
        tell(known.at[0], peers.y_near)
        tell(known.at[1], peers.x_near)
        tell(known.at[2], peers.z_near)
        has_below = jnp.where(peers.slab == 0, 0.0, 1.0)
        has_above = jnp.where(peers.slab == GROUPS * RING - 1, 0.0, 1.0)

    load_w.wait()
    taps = w_ref[...].astype(jnp.float32)

    def tap(s, u, k):
        at = ((s * 3 + u) * 3 + k) * CH
        return taps[at : at + CH]

    for s in range(3):
        pieces = [jnp.concatenate([tap(s, u, k) for k in range(3)], axis=1) for u in range(3)]
        banded(pieces, tf, s)

    def spread_volume(slot, values):
        xf[slot] = values.astype(jnp.float32).reshape(CH * ROWS, COLS)
        for row in range(ROWS):
            shifted(xf[slot, pl.ds(row, CH, stride=ROWS), :], xs, slot, row, False)

    if comm:
        for i in range(3):
            pl.semaphore_wait(known.at[i], 2)
        tell(known.at[3], peers.x_all)
        tell(known.at[4], peers.z_next)

    load_v.wait()
    for plane in range(PLANES):
        spread_volume(plane + 1, vown[:, plane])
    load_o.wait()
    load_u.wait()

    def activate(pre, slots, first, sides=(0, 1)):
        for side in sides:
            plane = slots[side] - 1
            for ch in range(CH):
                at = pl.ds(ch * ROWS, ROWS)
                value = pre[side, at, :] + off_ref[ch]
                sig = 0.5 * jnp.tanh(0.5 * value) + 0.5
                actn[ch, plane] = (value * sig).astype(jnp.bfloat16)
                grad = upn[ch, plane].astype(jnp.float32) * sig * (1.0 + value * (1.0 - sig))
                grad = grad.astype(jnp.bfloat16).astype(jnp.float32)
                pre[side, at, :] = grad
                row = jnp.sum(grad, axis=0, keepdims=True)
                if first and side == 0:
                    oacc[ch : ch + 1, :] = row
                else:
                    oacc[ch : ch + 1, :] += row
            for row in range(ROWS):
                shifted(pre[side, pl.ds(row, CH, stride=ROWS), :], gs, plane + 1, row, True)

    inner(xs, tf, pre_in)
    activate(pre_in, (2, 3), True)
    if comm:
        pl.semaphore_wait(known.at[3], 3)
        pl.semaphore_wait(known.at[4], 2)
        tell(known.at[5], [peers.twin])
    weight_terms(gs, xs, (2, 3), dacc, True)
    outer_own(xs, tf, pre_out)

    if comm:

        def edge(slot):
            return gs.at[slot, 1 : ROWS + 1, CH : 2 * CH, :]

        gup = remote(edge(PLANES), edge(0), gsend.at[0], grecv.at[0], peers.above)
        gdown = remote(edge(1), edge(PLANES + 1), gsend.at[1], grecv.at[1], peers.below)
        up_copy.wait_recv()
        spread_volume(0, vhalo[0].astype(jnp.float32) * has_below)
    else:
        for ref in (xs, gs):
            for slot in (0, PLANES + 1):
                ref[slot] = jnp.zeros_like(ref[slot])
    convolve(xs, tf, [(0, (0,))], (0,), pre_out, True)
    activate(pre_out, (1, 4), False, (0,))
    if comm:
        gdown.start()
        down_copy.wait_recv()
        spread_volume(PLANES + 1, vhalo[1].astype(jnp.float32) * has_above)
    convolve(xs, tf, [(2, (PLANES + 1,))], (1,), pre_out, True)
    activate(pre_out, (1, 4), False, (1,))
    if comm:
        gup.start()
    weight_terms(gs, xs, (1, 4), dacc, False)

    lane = lax.broadcasted_iota(jnp.int32, (PACKED, COLS), 1) // CH
    folded = dacc[...]
    folded = folded + pltpu.roll(folded, 2 * CH, 1)
    folded = folded + pltpu.roll(folded, CH, 1)
    packed = folded[:PACKED]
    for block in range(1, 4):
        packed = jnp.where(lane == block, folded[block * PACKED : (block + 1) * PACKED], packed)
    pay[:CHUNKS] = packed.reshape(CHUNKS, 8, COLS)
    pay[CHUNKS : CHUNKS + 4] = oacc[...].reshape(4, 8, COLS)
    pay[CHUNKS + 4 :] = jnp.zeros((MEMBERS - CHUNKS - 4, 8, COLS), jnp.float32)

    if comm:
        pl.semaphore_wait(known.at[5], 1)
        mine = peers.mine
        for other, peer in group:
            remote(pay.at[other], recv1.at[mine], rsend.at[0], rrecv.at[0], peer).start()
        recv1[mine] = pay[mine]

    turned = taps.T
    for s in range(3):
        pieces = []
        for u in range(3):
            at = ((2 - s) * 3 + 2 - u) * TAPS
            pieces.append(turned[:, at : at + TAPS])
        banded(pieces, tb, s)

    def finish(pre, slots):
        for side in range(2):
            gvn[:, slots[side] - 1] = pre[side].reshape(CH, ROWS, COLS).astype(jnp.bfloat16)

    inner(gs, tb, pre_in)

    if comm:
        some, few = pl.ds(0, MEMBERS - 1), pl.ds(0, RING - 1)
        pltpu.make_async_copy(recv1.at[some], recv1.at[some], rrecv.at[0]).wait()
        red[...] = jnp.sum(recv1[...], axis=0) * scale
        for other, peer in ring:
            remote(red, recv2.at[peers.z], rsend.at[1], rrecv.at[1], peer).start()
        recv2[peers.z] = red[...]

        finish(pre_in, (2, 3))
        outer_own(gs, tb, pre_out)
        gup.wait()
        gdown.wait()
        for slot, keep in ((0, has_below), (PLANES + 1, has_above)):
            for row in range(ROWS):
                value = gs[slot, row + 1, CH : 2 * CH, :].astype(jnp.float32) * keep
                shifted(value, gs, slot, row, True)

        pltpu.make_async_copy(recv2.at[few], recv2.at[few], rrecv.at[1]).wait()
        final[...] = jnp.sum(recv2[...], axis=0)
        for other, peer in group:
            remote(final, res.at[mine], rsend.at[2], rrecv.at[2], peer).start()
        res[mine] = final[...]
    else:
        finish(pre_in, (2, 3))
        outer_own(gs, tb, pre_out)
        res[...] = pay[...] * scale

    outer_halo(gs, tb, pre_out)
    finish(pre_out, (1, 4))
    if comm:
        up_copy.wait_send()
        down_copy.wait_send()
        pltpu.make_async_copy(recv1.at[some], recv1.at[some], rsend.at[0]).wait()
        pltpu.make_async_copy(recv2.at[few], recv2.at[few], rsend.at[1]).wait()
        pltpu.make_async_copy(recv1.at[some], recv1.at[some], rsend.at[2]).wait()
        pltpu.make_async_copy(recv1.at[some], recv1.at[some], rrecv.at[2]).wait()


def write_out(act_in, gvol_in, res, act, gvol, gk, go, gk_ref, go_ref, sem):
    pairs = ((act_in, act), (gvol_in, gvol), (gk_ref, gk), (go_ref, go))
    copies = [pltpu.make_async_copy(src, dst, sem.at[i]) for i, (src, dst) in enumerate(pairs)]
    copies[0].start()
    copies[1].start()
    full = res[:CHUNKS].reshape(PACKED, COLS)
    for block in range(4):
        moved = full if block == 0 else pltpu.roll(full, COLS - block * CH, 1)
        gk_ref[block * PACKED : (block + 1) * PACKED, :] = moved[:, :CH]
    copies[2].start()
    biases = res[CHUNKS : CHUNKS + 4].reshape(CH, COLS)
    go_ref[...] = jnp.sum(biases.T, axis=0, keepdims=True)
    copies[3].start()
    for copy in copies:
        copy.wait()


def layer(comm, scale, volume, kernel, offset, upstream):
    taps = jnp.transpose(kernel, (2, 3, 4, 0, 1)).reshape(27 * CH, CH)
    shape = (CH, PLANES, ROWS, COLS)
    wide = (PLANES + 2, ROWS + 2, TAPS, COLS)
    half, full = jnp.bfloat16, jnp.float32
    hbm = pl.BlockSpec(memory_space=pltpu.HBM)
    vmem = pl.BlockSpec(memory_space=pltpu.VMEM)
    act, gvol, res = pl.pallas_call(
        functools.partial(body, comm, scale),
        out_shape=(
            pltpu.VMEM(shape, half),
            pltpu.VMEM(shape, half),
            pltpu.VMEM((MEMBERS, 8, COLS), full),
        ),
        in_specs=[hbm, hbm, hbm, hbm],
        out_specs=(vmem, vmem, vmem),
        scratch_shapes=[
            pltpu.VMEM((27 * CH, CH), half),
            pltpu.SMEM((CH,), full),
            pltpu.VMEM(shape, half),
            pltpu.VMEM((2, CH, ROWS, COLS), half),
            pltpu.VMEM(shape, half),
            pltpu.VMEM((PLANES + 2, CH * ROWS, COLS), full),
            pltpu.VMEM(wide, half),
            pltpu.VMEM(wide, half),
            pltpu.VMEM((3, BLOCK * CH, DEEP), half),
            pltpu.VMEM((3, BLOCK * CH, DEEP), half),
            pltpu.VMEM((2, CH * ROWS, COLS), full),
            pltpu.VMEM((2, CH * ROWS, COLS), full),
            pltpu.VMEM((27 * CH, COLS), full),
            pltpu.VMEM((CH, COLS), full),
            pltpu.VMEM((MEMBERS, 8, COLS), full),
            pltpu.VMEM((MEMBERS, 8, COLS), full),
            pltpu.VMEM((8, COLS), full),
            pltpu.VMEM((RING, 8, COLS), full),
            pltpu.VMEM((8, COLS), full),
            pltpu.SemaphoreType.DMA((7,)),
            pltpu.SemaphoreType.DMA((2,)),
            pltpu.SemaphoreType.DMA((2,)),
            pltpu.SemaphoreType.DMA((2,)),
            pltpu.SemaphoreType.DMA((2,)),
            pltpu.SemaphoreType.DMA((3,)),
            pltpu.SemaphoreType.DMA((3,)),
            pltpu.SemaphoreType.REGULAR((6,)),
        ],
        compiler_params=pltpu.CompilerParams(
            vmem_limit_bytes=VMEM,
            **({"collective_id": 0, "has_side_effects": True} if comm else {}),
        ),
        cost_estimate=pl.CostEstimate(flops=10**10, bytes_accessed=4 * 10**6, transcendentals=10**6),
    )(volume.reshape(shape), taps, offset, upstream.reshape(shape))
    act, gvol, gk, go = pl.pallas_call(
        write_out,
        out_shape=(
            jax.ShapeDtypeStruct(shape, half),
            jax.ShapeDtypeStruct(shape, half),
            jax.ShapeDtypeStruct((27 * CH, CH), full),
            jax.ShapeDtypeStruct((1, CH), full),
        ),
        in_specs=[vmem, vmem, vmem],
        out_specs=(hbm, hbm, hbm, hbm),
        scratch_shapes=[
            pltpu.VMEM((27 * CH, CH), full),
            pltpu.VMEM((1, CH), full),
            pltpu.SemaphoreType.DMA((4,)),
        ],
        compiler_params=pltpu.CompilerParams(vmem_limit_bytes=8 * 1024 * 1024),
        cost_estimate=pl.CostEstimate(flops=10**5, bytes_accessed=3 * 10**6, transcendentals=0),
    )(act, gvol, res)
    return (
        act.reshape(volume.shape),
        gvol.reshape(volume.shape),
        jnp.transpose(gk.reshape(3, 3, 3, CH, CH), (3, 4, 0, 1, 2)),
        go.reshape(CH),
    )


def solution(mesh):
    cells = mesh.shape["batch"] * mesh.shape["slab"] * PLANES * ROWS * COLS
    split = P("batch", None, "slab", None, None)
    return jax.shard_map(
        functools.partial(layer, True, cells**-0.5),
        mesh=mesh,
        in_specs=(split, P(), P(), split),
        out_specs=(split, split, P(), P()),
        check_vma=False,
    )
```

```python
import functools

import jax
import jax.numpy as jnp
from jax import lax
from jax.experimental import pallas as pl
from jax.experimental.pallas import tpu as pltpu
from jax.sharding import PartitionSpec as P

MESH = pl.DeviceIdType.MESH
VMEM = 65_500_000
CH = 32
PLANES = 4
ROWS = 16
COLS = 128
BLOCK = 8
WIN = BLOCK + 2
TAPS = 3 * CH
DEEP = 1024
GROUPS = 4
RING = 8
MEMBERS = 8 * GROUPS
PACKED = 27 * CH // 4
CHUNKS = PACKED // 8


def banded(pieces, out_ref, plane):
    whole = jnp.concatenate(pieces, axis=1)
    for row in range(BLOCK):
        parts = [whole]
        if row > 0:
            parts.insert(0, jnp.zeros((CH, row * TAPS), jnp.float32))
        parts.append(jnp.zeros((CH, DEEP - (row + 3) * TAPS), jnp.float32))
        block = jnp.concatenate(parts, axis=1)
        out_ref[row * CH : (row + 1) * CH, plane * DEEP : (plane + 1) * DEEP] = block.astype(
            jnp.bfloat16
        )


def shifted(values, out_ref, slot, row, flip):
    lane = lax.broadcasted_iota(jnp.int32, (CH, COLS), 1)
    left = jnp.where(lane == 0, 0.0, pltpu.roll(values, 1, 1))
    right = jnp.where(lane == COLS - 1, 0.0, pltpu.roll(values, COLS - 1, 1))
    if flip:
        left, right = right, left
    out_ref[slot, row + 1, 0:CH, :] = left.astype(jnp.bfloat16)
    out_ref[slot, row + 1, CH : 2 * CH, :] = values.astype(jnp.bfloat16)
    out_ref[slot, row + 1, 2 * CH : 3 * CH, :] = right.astype(jnp.bfloat16)


def clear_edges(ref):
    zero = jnp.zeros((TAPS, COLS), jnp.bfloat16)
    for slot in range(PLANES + 2):
        ref[slot, 0] = zero
        ref[slot, ROWS + 1] = zero


def window(ref, slot, half):
    rows = ref[slot, half * BLOCK : half * BLOCK + WIN].reshape(WIN * TAPS, COLS)
    return jnp.concatenate([rows, jnp.zeros((DEEP - WIN * TAPS, COLS), jnp.bfloat16)], axis=0)


def product(src_ref, t_ref, first, slots, half):
    sides = [jnp.concatenate([window(src_ref, s, half) for s in group], axis=0) for group in slots]
    columns = slice(first * DEEP, (first + len(slots[0])) * DEEP)
    rhs = jnp.concatenate(sides, axis=1)
    return jnp.dot(t_ref[:, columns], rhs, preferred_element_type=jnp.float32)


def put(out_ref, side, half, value, add):
    for row in range(BLOCK):
        at = pl.ds(half * BLOCK + row, CH, stride=ROWS)
        part = value[row * CH : (row + 1) * CH]
        out_ref[side, at, :] = part + out_ref[side, at, :] if add else part


def inner(src_ref, t_ref, out_ref):
    for half in range(ROWS // BLOCK):
        acc = product(src_ref, t_ref, 0, [(1, 2, 3), (2, 3, 4)], half)
        put(out_ref, 0, half, acc[:, :COLS], False)
        put(out_ref, 1, half, acc[:, COLS:], False)


def outer_own(src_ref, t_ref, out_ref):
    for half in range(ROWS // BLOCK):
        both = product(src_ref, t_ref, 1, [(1,), (PLANES,)], half)
        low = both[:, :COLS] + product(src_ref, t_ref, 2, [(2,)], half)
        high = both[:, COLS:] + product(src_ref, t_ref, 0, [(PLANES - 1,)], half)
        put(out_ref, 0, half, low, False)
        put(out_ref, 1, half, high, False)


def outer_halo(src_ref, t_ref, out_ref, side):
    first, slot = (0, 0) if side == 0 else (2, PLANES + 1)
    for half in range(ROWS // BLOCK):
        put(out_ref, side, half, product(src_ref, t_ref, first, [(slot,)], half), True)


def weight_terms(gs_ref, xs_ref, pair, dacc_ref, first):
    lhs, rhs = [], []
    pad = jnp.ones((CH * 2, COLS), jnp.bfloat16)
    for row in range(0, ROWS, 2):
        for slot in pair:
            lhs.append(gs_ref[slot, row : row + 4].reshape(4 * TAPS, COLS))
            sides = [
                xs_ref[slot + s - 1, row + 1 : row + 3, CH : 2 * CH, :].reshape(2 * CH, COLS)
                for s in range(3)
            ]
            rhs.append(jnp.concatenate(sides + [pad], axis=0))
    prod = lax.dot_general(
        jnp.concatenate(lhs, axis=1),
        jnp.concatenate(rhs, axis=1),
        (((1,), (1,)), ((), ())),
        preferred_element_type=jnp.float32,
    )
    if first:
        dacc_ref[...] = prod
    else:
        dacc_ref[...] += prod


def pack(total):
    block = lax.broadcasted_iota(jnp.int32, (TAPS, COLS), 1) // CH
    sides = []
    for side in range(2):
        rows = []
        for kh in range(3):
            even = total[(2 - kh) * TAPS : (3 - kh) * TAPS, side * COLS : (side + 1) * COLS]
            odd = total[(3 - kh) * TAPS : (4 - kh) * TAPS, side * COLS : (side + 1) * COLS]
            rows.append(jnp.where(block % 2 == 0, even, odd))
        value = jnp.concatenate(rows, axis=0)
        sides.append(value + pltpu.roll(value, CH, 1))
    block = lax.broadcasted_iota(jnp.int32, (3 * TAPS, COLS), 1) // CH
    value = jnp.where(block == 0, pltpu.roll(sides[1], 3 * CH, 1), sides[0])
    rest = value[PACKED:]
    moved = [pltpu.roll(rest, shift * CH, 1) for shift in (1, 3, 2)]
    return jnp.where(block[:PACKED] == 2, jnp.concatenate(moved, axis=0), value[:PACKED])


def unpack(full, out_ref):
    rest = pltpu.roll(full, 2 * CH, 1)[:, :CH]
    for s, shift in enumerate((3, 1, 0)):
        at = s * 3 * TAPS
        value = full if shift == 0 else pltpu.roll(full, shift * CH, 1)
        out_ref[at : at + PACKED, :] = value[:, :CH]
        few = 3 * TAPS - PACKED
        out_ref[at + PACKED : at + 3 * TAPS, :] = rest[s * few : (s + 1) * few]


class Peers:
    def __init__(self):
        self.batch, self.slab = lax.axis_index("batch"), lax.axis_index("slab")
        self.y, self.z = self.slab // RING, self.slab % RING
        x, core = self.batch // 2, self.batch % 2
        self.mine = self.batch * GROUPS + self.y
        xs = [wrapped(x + d, 4) for d in range(4)]
        cores = [core, 1 - core]
        ys = [wrapped(self.y + d, GROUPS) for d in range(GROUPS)]
        zs = [wrapped(self.z + d, RING) for d in range(RING)]
        group = [(dx, dy, dc) for dx in range(4) for dy in range(GROUPS) for dc in range(2)]
        group = sorted(group[1:], key=lambda t: -(min(t[0], 4 - t[0]) + min(t[1], GROUPS - t[1])))
        self.group = []
        for dx, dy, dc in group:
            batch = xs[dx] * 2 + cores[dc]
            self.group.append((batch * GROUPS + ys[dy], (batch, ys[dy] * RING + self.z)))
        ring = sorted(range(1, RING), key=lambda d: -min(d, RING - d))
        self.ring = [(zs[d], (self.batch, self.y * RING + zs[d])) for d in ring]

        def place(dx=0, dy=0, dz=0, dc=0):
            return (xs[dx] * 2 + cores[dc], ys[dy] * RING + zs[dz])

        self.x_near = [place(dx=1), place(dx=3)]
        self.x_all = [place(dx=1), place(dx=3), place(dx=2)]
        self.y_near = [place(dy=1), place(dy=GROUPS - 1)]
        self.z_near = [place(dz=1), place(dz=RING - 1)]
        self.z_next = [place(dz=2), place(dz=RING - 2)]
        self.twin = place(dc=1)
        self.above = (self.batch, wrapped(self.slab + 1, GROUPS * RING))
        self.below = (self.batch, wrapped(self.slab + GROUPS * RING - 1, GROUPS * RING))


def wrapped(value, count):
    return jnp.where(value >= count, value - count, value)


def remote(src, dst, send, recv, peer):
    return pltpu.make_async_remote_copy(src, dst, send, recv, peer, MESH)


def tell(sem, peers):
    for peer in peers:
        pl.semaphore_signal(sem, 1, device_id=peer, device_id_type=MESH)


def body(
    comm,
    scale,
    vol,
    w_hbm,
    off_hbm,
    up,
    actn,
    gvn,
    res,
    w_ref,
    off_ref,
    vown,
    vhalo,
    upn,
    xf,
    xs,
    gs,
    tf,
    tb,
    pre_in,
    pre_out,
    dacc,
    pay,
    recv1,
    red,
    recv2,
    final,
    local_sem,
    vsend,
    vrecv,
    gsend,
    grecv,
    rsend,
    rrecv,
    known,
):
    if comm:
        peers = Peers()
        group, ring = peers.group, peers.ring
        barrier = pltpu.get_barrier_semaphore()
        near = [peers.above, peers.below] + peers.z_near + peers.y_near + peers.x_near
        near.append(peers.twin)
        tell(barrier, near)

    load_w = pltpu.make_async_copy(w_hbm, w_ref, local_sem.at[4])
    load_w.start()
    load_v = pltpu.make_async_copy(vol, vown, local_sem.at[0])
    load_v.start()
    load_o = pltpu.make_async_copy(off_hbm, off_ref, local_sem.at[5])
    load_o.start()
    load_u = pltpu.make_async_copy(up, upn, local_sem.at[1])
    load_u.start()
    clear_edges(xs)
    clear_edges(gs)

    if comm:
        pl.semaphore_wait(barrier, len(near))
        up_copy = remote(vol.at[:, PLANES - 1], vhalo.at[0], vsend.at[0], vrecv.at[0], peers.above)
        down_copy = remote(vol.at[:, 0], vhalo.at[1], vsend.at[1], vrecv.at[1], peers.below)
        up_copy.start()
        down_copy.start()
        tell(known.at[0], peers.y_near)
        tell(known.at[1], peers.x_near)
        tell(known.at[2], peers.z_near)
        has_below = jnp.where(peers.slab == 0, 0.0, 1.0)
        has_above = jnp.where(peers.slab == GROUPS * RING - 1, 0.0, 1.0)

    load_w.wait()
    taps = w_ref[...].astype(jnp.float32)

    def tap(s, u, k):
        at = ((s * 3 + u) * 3 + k) * CH
        return taps[at : at + CH]

    for s in range(3):
        pieces = [jnp.concatenate([tap(s, u, k) for k in range(3)], axis=1) for u in range(3)]
        banded(pieces, tf, s)

    def spread_volume(slot, values):
        xf[slot] = values.astype(jnp.float32).reshape(CH * ROWS, COLS)
        for row in range(ROWS):
            shifted(xf[slot, pl.ds(row, CH, stride=ROWS), :], xs, slot, row, False)

    if comm:
        for i in range(3):
            pl.semaphore_wait(known.at[i], 2)
        tell(known.at[3], peers.x_all)
        tell(known.at[4], peers.z_next)

    load_v.wait()
    for plane in range(PLANES):
        spread_volume(plane + 1, vown[:, plane])
    load_o.wait()
    load_u.wait()

    def activate(pre, slots, sides):
        for side in sides:
            plane = slots[side] - 1
            for ch in range(CH):
                at = pl.ds(ch * ROWS, ROWS)
                value = pre[side, at, :] + off_ref[ch]
                sig = 0.5 * jnp.tanh(0.5 * value) + 0.5
                actn[ch, plane] = (value * sig).astype(jnp.bfloat16)
                grad = upn[ch, plane].astype(jnp.float32) * sig * (1.0 + value * (1.0 - sig))
                pre[side, at, :] = grad
            for row in range(ROWS):
                shifted(pre[side, pl.ds(row, CH, stride=ROWS), :], gs, plane + 1, row, True)

    inner(xs, tf, pre_in)
    activate(pre_in, (2, 3), (0, 1))
    if comm:
        pl.semaphore_wait(known.at[3], 3)
        pl.semaphore_wait(known.at[4], 2)
        tell(known.at[5], [peers.twin])
    weight_terms(gs, xs, (2, 3), dacc, True)
    outer_own(xs, tf, pre_out)

    if comm:

        def edge(slot):
            return gs.at[slot, 1 : ROWS + 1, CH : 2 * CH, :]

        gup = remote(edge(PLANES), edge(0), gsend.at[0], grecv.at[0], peers.above)
        gdown = remote(edge(1), edge(PLANES + 1), gsend.at[1], grecv.at[1], peers.below)
        up_copy.wait_recv()
        spread_volume(0, vhalo[0].astype(jnp.float32) * has_below)
    else:
        for ref in (xs, gs):
            for slot in (0, PLANES + 1):
                ref[slot] = jnp.zeros_like(ref[slot])
    outer_halo(xs, tf, pre_out, 0)
    activate(pre_out, (1, 4), (0,))
    if comm:
        gdown.start()
        down_copy.wait_recv()
        spread_volume(PLANES + 1, vhalo[1].astype(jnp.float32) * has_above)
    outer_halo(xs, tf, pre_out, 1)
    activate(pre_out, (1, 4), (1,))
    if comm:
        gup.start()
    weight_terms(gs, xs, (1, 4), dacc, False)

    packed = pack(dacc[...])
    pay[:CHUNKS] = packed.reshape(CHUNKS, 8, COLS)
    sums = [dacc[row * TAPS + CH : row * TAPS + 2 * CH, COLS:] for row in (1, 2)]
    pay[CHUNKS : CHUNKS + 4] = (sums[0] + sums[1]).reshape(4, 8, COLS)
    pay[CHUNKS + 4 :] = jnp.zeros((MEMBERS - CHUNKS - 4, 8, COLS), jnp.float32)

    if comm:
        pl.semaphore_wait(known.at[5], 1)
        mine = peers.mine
        for other, peer in group:
            remote(pay.at[other], recv1.at[mine], rsend.at[0], rrecv.at[0], peer).start()
        recv1[mine] = pay[mine]

    turned = taps.T
    for s in range(3):
        pieces = []
        for u in range(3):
            at = ((2 - s) * 3 + 2 - u) * TAPS
            pieces.append(turned[:, at : at + TAPS])
        banded(pieces, tb, s)

    def finish(pre, slots):
        for side in range(2):
            gvn[:, slots[side] - 1] = pre[side].reshape(CH, ROWS, COLS).astype(jnp.bfloat16)

    inner(gs, tb, pre_in)

    if comm:
        some, few = pl.ds(0, MEMBERS - 1), pl.ds(0, RING - 1)
        pltpu.make_async_copy(recv1.at[some], recv1.at[some], rrecv.at[0]).wait()
        red[...] = jnp.sum(recv1[...], axis=0) * scale
        for other, peer in ring:
            remote(red, recv2.at[peers.z], rsend.at[1], rrecv.at[1], peer).start()
        recv2[peers.z] = red[...]

        finish(pre_in, (2, 3))
        outer_own(gs, tb, pre_out)
        gup.wait()
        gdown.wait()
        for slot, keep in ((0, has_below), (PLANES + 1, has_above)):
            for row in range(ROWS):
                value = gs[slot, row + 1, CH : 2 * CH, :].astype(jnp.float32) * keep
                shifted(value, gs, slot, row, True)

        pltpu.make_async_copy(recv2.at[few], recv2.at[few], rrecv.at[1]).wait()
        final[...] = jnp.sum(recv2[...], axis=0)
        for other, peer in group:
            remote(final, res.at[mine], rsend.at[2], rrecv.at[2], peer).start()
        res[mine] = final[...]
    else:
        finish(pre_in, (2, 3))
        outer_own(gs, tb, pre_out)
        res[...] = pay[...] * scale

    outer_halo(gs, tb, pre_out, 0)
    outer_halo(gs, tb, pre_out, 1)
    finish(pre_out, (1, 4))
    if comm:
        up_copy.wait_send()
        down_copy.wait_send()
        pltpu.make_async_copy(recv1.at[some], recv1.at[some], rsend.at[0]).wait()
        pltpu.make_async_copy(recv2.at[few], recv2.at[few], rsend.at[1]).wait()
        pltpu.make_async_copy(recv1.at[some], recv1.at[some], rsend.at[2]).wait()
        pltpu.make_async_copy(recv1.at[some], recv1.at[some], rrecv.at[2]).wait()


def write_out(act_in, gvol_in, res, act, gvol, gk, go, gk_ref, go_ref, sem):
    pairs = ((act_in, act), (gvol_in, gvol), (gk_ref, gk), (go_ref, go))
    copies = [pltpu.make_async_copy(src, dst, sem.at[i]) for i, (src, dst) in enumerate(pairs)]
    copies[0].start()
    copies[1].start()
    unpack(res[:CHUNKS].reshape(PACKED, COLS), gk_ref)
    copies[2].start()
    biases = res[CHUNKS : CHUNKS + 4].reshape(CH, COLS)
    go_ref[...] = biases.T[2 * CH : 2 * CH + 1, :]
    copies[3].start()
    for copy in copies:
        copy.wait()


def layer(comm, scale, volume, kernel, offset, upstream):
    taps = jnp.transpose(kernel, (2, 3, 4, 0, 1)).reshape(27 * CH, CH)
    shape = (CH, PLANES, ROWS, COLS)
    wide = (PLANES + 2, ROWS + 2, TAPS, COLS)
    half, full = jnp.bfloat16, jnp.float32
    hbm = pl.BlockSpec(memory_space=pltpu.HBM)
    vmem = pl.BlockSpec(memory_space=pltpu.VMEM)
    act, gvol, res = pl.pallas_call(
        functools.partial(body, comm, scale),
        out_shape=(
            pltpu.VMEM(shape, half),
            pltpu.VMEM(shape, half),
            pltpu.VMEM((MEMBERS, 8, COLS), full),
        ),
        in_specs=[hbm, hbm, hbm, hbm],
        out_specs=(vmem, vmem, vmem),
        scratch_shapes=[
            pltpu.VMEM((27 * CH, CH), half),
            pltpu.SMEM((CH,), full),
            pltpu.VMEM(shape, half),
            pltpu.VMEM((2, CH, ROWS, COLS), half),
            pltpu.VMEM(shape, half),
            pltpu.VMEM((PLANES + 2, CH * ROWS, COLS), full),
            pltpu.VMEM(wide, half),
            pltpu.VMEM(wide, half),
            pltpu.VMEM((BLOCK * CH, 3 * DEEP), half),
            pltpu.VMEM((BLOCK * CH, 3 * DEEP), half),
            pltpu.VMEM((2, CH * ROWS, COLS), full),
            pltpu.VMEM((2, CH * ROWS, COLS), full),
            pltpu.VMEM((4 * TAPS, 2 * COLS), full),
            pltpu.VMEM((MEMBERS, 8, COLS), full),
            pltpu.VMEM((MEMBERS, 8, COLS), full),
            pltpu.VMEM((8, COLS), full),
            pltpu.VMEM((RING, 8, COLS), full),
            pltpu.VMEM((8, COLS), full),
            pltpu.SemaphoreType.DMA((7,)),
            pltpu.SemaphoreType.DMA((2,)),
            pltpu.SemaphoreType.DMA((2,)),
            pltpu.SemaphoreType.DMA((2,)),
            pltpu.SemaphoreType.DMA((2,)),
            pltpu.SemaphoreType.DMA((3,)),
            pltpu.SemaphoreType.DMA((3,)),
            pltpu.SemaphoreType.REGULAR((6,)),
        ],
        compiler_params=pltpu.CompilerParams(
            vmem_limit_bytes=VMEM,
            **({"collective_id": 0, "has_side_effects": True} if comm else {}),
        ),
        cost_estimate=pl.CostEstimate(flops=10**10, bytes_accessed=4 * 10**6, transcendentals=10**6),
    )(volume.reshape(shape), taps, offset, upstream.reshape(shape))
    act, gvol, gk, go = pl.pallas_call(
        write_out,
        out_shape=(
            jax.ShapeDtypeStruct(shape, half),
            jax.ShapeDtypeStruct(shape, half),
            jax.ShapeDtypeStruct((27 * CH, CH), full),
            jax.ShapeDtypeStruct((1, CH), full),
        ),
        in_specs=[vmem, vmem, vmem],
        out_specs=(hbm, hbm, hbm, hbm),
        scratch_shapes=[
            pltpu.VMEM((27 * CH, CH), full),
            pltpu.VMEM((1, CH), full),
            pltpu.SemaphoreType.DMA((4,)),
        ],
        compiler_params=pltpu.CompilerParams(vmem_limit_bytes=8 * 1024 * 1024),
        cost_estimate=pl.CostEstimate(flops=10**5, bytes_accessed=3 * 10**6, transcendentals=0),
    )(act, gvol, res)
    return (
        act.reshape(volume.shape),
        gvol.reshape(volume.shape),
        jnp.transpose(gk.reshape(3, 3, 3, CH, CH), (3, 4, 0, 1, 2)),
        go.reshape(CH),
    )


def solution(mesh):
    cells = mesh.shape["batch"] * mesh.shape["slab"] * PLANES * ROWS * COLS
    split = P("batch", None, "slab", None, None)
    return jax.shard_map(
        functools.partial(layer, True, cells**-0.5),
        mesh=mesh,
        in_specs=(split, P(), P(), split),
        out_specs=(split, split, P(), P()),
        check_vma=False,
    )
```

```python
import functools

import jax
import jax.numpy as jnp
from jax import lax
from jax.experimental import pallas as pl
from jax.experimental.pallas import tpu as pltpu
from jax.sharding import PartitionSpec as P

MESH = pl.DeviceIdType.MESH
VMEM = 65_500_000
CH = 32
PLANES = 4
ROWS = 16
COLS = 128
BLOCK = 8
WIN = BLOCK + 2
TAPS = 3 * CH
DEEP = 1024
GROUPS = 4
RING = 8
MEMBERS = 8 * GROUPS
PACKED = 27 * CH // 4
CHUNKS = PACKED // 8


def banded(pieces, out_ref, plane):
    whole = jnp.concatenate(pieces, axis=1)
    for row in range(BLOCK):
        parts = [whole]
        if row > 0:
            parts.insert(0, jnp.zeros((CH, row * TAPS), jnp.float32))
        parts.append(jnp.zeros((CH, DEEP - (row + 3) * TAPS), jnp.float32))
        block = jnp.concatenate(parts, axis=1)
        out_ref[row * CH : (row + 1) * CH, plane * DEEP : (plane + 1) * DEEP] = block.astype(
            jnp.bfloat16
        )


def shifted(values, out_ref, slot, row, flip):
    lane = lax.broadcasted_iota(jnp.int32, (CH, COLS), 1)
    left = jnp.where(lane == 0, 0.0, pltpu.roll(values, 1, 1))
    right = jnp.where(lane == COLS - 1, 0.0, pltpu.roll(values, COLS - 1, 1))
    if flip:
        left, right = right, left
    out_ref[slot, row + 1, 0:CH, :] = left.astype(jnp.bfloat16)
    out_ref[slot, row + 1, CH : 2 * CH, :] = values.astype(jnp.bfloat16)
    out_ref[slot, row + 1, 2 * CH : 3 * CH, :] = right.astype(jnp.bfloat16)


def clear_edges(ref):
    zero = jnp.zeros((TAPS, COLS), jnp.bfloat16)
    for slot in range(PLANES + 2):
        ref[slot, 0] = zero
        ref[slot, ROWS + 1] = zero


def window(ref, slot, half):
    rows = ref[slot, half * BLOCK : half * BLOCK + WIN].reshape(WIN * TAPS, COLS)
    return jnp.concatenate([rows, jnp.zeros((DEEP - WIN * TAPS, COLS), jnp.bfloat16)], axis=0)


def product(src_ref, t_ref, first, slots, half):
    sides = [jnp.concatenate([window(src_ref, s, half) for s in group], axis=0) for group in slots]
    columns = slice(first * DEEP, (first + len(slots[0])) * DEEP)
    rhs = jnp.concatenate(sides, axis=1)
    return jnp.dot(t_ref[:, columns], rhs, preferred_element_type=jnp.float32)


def put(out_ref, side, half, value, add):
    for row in range(BLOCK):
        at = pl.ds(half * BLOCK + row, CH, stride=ROWS)
        part = value[row * CH : (row + 1) * CH]
        out_ref[side, at, :] = part + out_ref[side, at, :] if add else part


def inner(src_ref, t_ref, out_ref):
    for half in range(ROWS // BLOCK):
        acc = product(src_ref, t_ref, 0, [(1, 2, 3), (2, 3, 4)], half)
        put(out_ref, 0, half, acc[:, :COLS], False)
        put(out_ref, 1, half, acc[:, COLS:], False)


def outer_own(src_ref, t_ref, out_ref):
    for half in range(ROWS // BLOCK):
        both = product(src_ref, t_ref, 1, [(1,), (PLANES,)], half)
        low = both[:, :COLS] + product(src_ref, t_ref, 2, [(2,)], half)
        high = both[:, COLS:] + product(src_ref, t_ref, 0, [(PLANES - 1,)], half)
        put(out_ref, 0, half, low, False)
        put(out_ref, 1, half, high, False)


def outer_halo(src_ref, t_ref, out_ref, side):
    first, slot = (0, 0) if side == 0 else (2, PLANES + 1)
    for half in range(ROWS // BLOCK):
        put(out_ref, side, half, product(src_ref, t_ref, first, [(slot,)], half), True)


def weight_terms(gs_ref, xs_ref, pair, dacc_ref, first):
    lhs, rhs = [], []
    pad = jnp.ones((CH * 2, COLS), jnp.bfloat16)
    for row in range(0, ROWS, 2):
        for slot in pair:
            lhs.append(gs_ref[slot, row : row + 4].reshape(4 * TAPS, COLS))
            sides = [
                xs_ref[slot + s - 1, row + 1 : row + 3, CH : 2 * CH, :].reshape(2 * CH, COLS)
                for s in range(3)
            ]
            rhs.append(jnp.concatenate(sides + [pad], axis=0))
    prod = lax.dot_general(
        jnp.concatenate(lhs, axis=1),
        jnp.concatenate(rhs, axis=1),
        (((1,), (1,)), ((), ())),
        preferred_element_type=jnp.float32,
    )
    if first:
        dacc_ref[...] = prod
    else:
        dacc_ref[...] += prod


def pack(total):
    block = lax.broadcasted_iota(jnp.int32, (TAPS, COLS), 1) // CH
    sides = []
    for side in range(2):
        rows = []
        for kh in range(3):
            even = total[(2 - kh) * TAPS : (3 - kh) * TAPS, side * COLS : (side + 1) * COLS]
            odd = total[(3 - kh) * TAPS : (4 - kh) * TAPS, side * COLS : (side + 1) * COLS]
            rows.append(jnp.where(block % 2 == 0, even, odd))
        value = jnp.concatenate(rows, axis=0)
        sides.append(value + pltpu.roll(value, CH, 1))
    block = lax.broadcasted_iota(jnp.int32, (3 * TAPS, COLS), 1) // CH
    value = jnp.where(block == 0, pltpu.roll(sides[1], 3 * CH, 1), sides[0])
    rest = value[PACKED:]
    moved = [pltpu.roll(rest, shift * CH, 1) for shift in (1, 3, 2)]
    return jnp.where(block[:PACKED] == 2, jnp.concatenate(moved, axis=0), value[:PACKED])


def unpack(full, out_ref):
    rest = pltpu.roll(full, 2 * CH, 1)[:, :CH]
    for s, shift in enumerate((3, 1, 0)):
        at = s * 3 * TAPS
        value = full if shift == 0 else pltpu.roll(full, shift * CH, 1)
        out_ref[at : at + PACKED, :] = value[:, :CH]
        few = 3 * TAPS - PACKED
        out_ref[at + PACKED : at + 3 * TAPS, :] = rest[s * few : (s + 1) * few]


class Peers:
    def __init__(self):
        self.batch, self.slab = lax.axis_index("batch"), lax.axis_index("slab")
        self.y, self.z = self.slab // RING, self.slab % RING
        x, core = self.batch // 2, self.batch % 2
        self.mine = self.batch * GROUPS + self.y
        xs = [wrapped(x + d, 4) for d in range(4)]
        cores = [core, 1 - core]
        ys = [wrapped(self.y + d, GROUPS) for d in range(GROUPS)]
        zs = [wrapped(self.z + d, RING) for d in range(RING)]
        group = [(dx, dy, dc) for dx in range(4) for dy in range(GROUPS) for dc in range(2)]
        group = sorted(group[1:], key=lambda t: -(min(t[0], 4 - t[0]) + min(t[1], GROUPS - t[1])))
        self.group = []
        for dx, dy, dc in group:
            batch = xs[dx] * 2 + cores[dc]
            self.group.append((batch * GROUPS + ys[dy], (batch, ys[dy] * RING + self.z)))
        ring = sorted(range(1, RING), key=lambda d: -min(d, RING - d))
        self.ring = [(zs[d], (self.batch, self.y * RING + zs[d])) for d in ring]

        def place(dx=0, dy=0, dz=0, dc=0):
            return (xs[dx] * 2 + cores[dc], ys[dy] * RING + zs[dz])

        self.x_near = [place(dx=1), place(dx=3)]
        self.x_all = [place(dx=1), place(dx=3), place(dx=2)]
        self.y_near = [place(dy=1), place(dy=GROUPS - 1)]
        self.z_near = [place(dz=1), place(dz=RING - 1)]
        self.z_next = [place(dz=2), place(dz=RING - 2)]
        self.twin = place(dc=1)
        self.above = (self.batch, wrapped(self.slab + 1, GROUPS * RING))
        self.below = (self.batch, wrapped(self.slab + GROUPS * RING - 1, GROUPS * RING))


def wrapped(value, count):
    return jnp.where(value >= count, value - count, value)


def remote(src, dst, send, recv, peer):
    return pltpu.make_async_remote_copy(src, dst, send, recv, peer, MESH)


def tell(sem, peers):
    for peer in peers:
        pl.semaphore_signal(sem, 1, device_id=peer, device_id_type=MESH)


def body(
    comm,
    scale,
    vol,
    w_hbm,
    off_hbm,
    up,
    actn,
    gvn,
    res,
    w_ref,
    off_ref,
    vown,
    vhalo,
    upn,
    xf,
    xs,
    gs,
    tf,
    tb,
    pre_in,
    pre_out,
    dacc,
    pay,
    recv1,
    red,
    recv2,
    final,
    local_sem,
    vsend,
    vrecv,
    gsend,
    grecv,
    rsend,
    rrecv,
    known,
):
    if comm:
        peers = Peers()
        group, ring = peers.group, peers.ring
        barrier = pltpu.get_barrier_semaphore()
        near = [peers.above, peers.below] + peers.z_near + peers.y_near + peers.x_near
        near.append(peers.twin)
        tell(barrier, near)

    load_w = pltpu.make_async_copy(w_hbm, w_ref, local_sem.at[4])
    load_w.start()
    load_v = pltpu.make_async_copy(vol, vown, local_sem.at[0])
    load_v.start()
    load_o = pltpu.make_async_copy(off_hbm, off_ref, local_sem.at[5])
    load_o.start()
    load_u = pltpu.make_async_copy(up, upn, local_sem.at[1])
    load_u.start()
    clear_edges(xs)
    clear_edges(gs)

    if comm:
        pl.semaphore_wait(barrier, len(near))
        up_copy = remote(vol.at[:, PLANES - 1], vhalo.at[0], vsend.at[0], vrecv.at[0], peers.above)
        down_copy = remote(vol.at[:, 0], vhalo.at[1], vsend.at[1], vrecv.at[1], peers.below)
        up_copy.start()
        down_copy.start()
        tell(known.at[0], peers.y_near)
        tell(known.at[1], peers.x_near)
        tell(known.at[2], peers.z_near)
        has_below = jnp.where(peers.slab == 0, 0.0, 1.0)
        has_above = jnp.where(peers.slab == GROUPS * RING - 1, 0.0, 1.0)

    load_w.wait()
    taps = w_ref[...].astype(jnp.float32)

    def tap(s, u, k):
        at = ((s * 3 + u) * 3 + k) * CH
        return taps[at : at + CH]

    for s in range(3):
        pieces = [jnp.concatenate([tap(s, u, k) for k in range(3)], axis=1) for u in range(3)]
        banded(pieces, tf, s)

    def spread_volume(slot, values):
        xf[slot] = values.astype(jnp.float32).reshape(CH * ROWS, COLS)
        for row in range(ROWS):
            shifted(xf[slot, pl.ds(row, CH, stride=ROWS), :], xs, slot, row, False)

    load_v.wait()
    for plane in range(PLANES):
        spread_volume(plane + 1, vown[:, plane])
    load_o.wait()
    load_u.wait()

    def activate(pre, slots, sides):
        for side in sides:
            plane = slots[side] - 1
            for ch in range(CH):
                at = pl.ds(ch * ROWS, ROWS)
                value = pre[side, at, :] + off_ref[ch]
                sig = 0.5 * jnp.tanh(0.5 * value) + 0.5
                actn[ch, plane] = (value * sig).astype(jnp.bfloat16)
                grad = upn[ch, plane].astype(jnp.float32) * sig * (1.0 + value * (1.0 - sig))
                pre[side, at, :] = grad
            for row in range(ROWS):
                shifted(pre[side, pl.ds(row, CH, stride=ROWS), :], gs, plane + 1, row, True)

    inner(xs, tf, pre_in)
    if comm:
        for i in range(3):
            pl.semaphore_wait(known.at[i], 2)
        tell(known.at[3], peers.x_all)
        tell(known.at[4], peers.z_next)
    activate(pre_in, (2, 3), (0, 1))
    weight_terms(gs, xs, (2, 3), dacc, True)
    outer_own(xs, tf, pre_out)
    if comm:
        pl.semaphore_wait(known.at[3], 3)
        pl.semaphore_wait(known.at[4], 2)
        tell(known.at[5], [peers.twin])

    if comm:

        def edge(slot):
            return gs.at[slot, 1 : ROWS + 1, CH : 2 * CH, :]

        gup = remote(edge(PLANES), edge(0), gsend.at[0], grecv.at[0], peers.above)
        gdown = remote(edge(1), edge(PLANES + 1), gsend.at[1], grecv.at[1], peers.below)
        up_copy.wait_recv()
        spread_volume(0, vhalo[0].astype(jnp.float32) * has_below)
    else:
        for ref in (xs, gs):
            for slot in (0, PLANES + 1):
                ref[slot] = jnp.zeros_like(ref[slot])
    outer_halo(xs, tf, pre_out, 0)
    activate(pre_out, (1, 4), (0,))
    if comm:
        gdown.start()
        down_copy.wait_recv()
        spread_volume(PLANES + 1, vhalo[1].astype(jnp.float32) * has_above)
    outer_halo(xs, tf, pre_out, 1)
    activate(pre_out, (1, 4), (1,))
    if comm:
        gup.start()
    weight_terms(gs, xs, (1, 4), dacc, False)

    packed = pack(dacc[...])
    pay[:CHUNKS] = packed.reshape(CHUNKS, 8, COLS)
    sums = [dacc[row * TAPS + CH : row * TAPS + 2 * CH, COLS:] for row in (1, 2)]
    pay[CHUNKS : CHUNKS + 4] = (sums[0] + sums[1]).reshape(4, 8, COLS)
    pay[CHUNKS + 4 :] = jnp.zeros((MEMBERS - CHUNKS - 4, 8, COLS), jnp.float32)

    if comm:
        pl.semaphore_wait(known.at[5], 1)
        mine = peers.mine
        for other, peer in group:
            remote(pay.at[other], recv1.at[mine], rsend.at[0], rrecv.at[0], peer).start()
        recv1[mine] = pay[mine]

    turned = taps.T
    for s in range(3):
        pieces = []
        for u in range(3):
            at = ((2 - s) * 3 + 2 - u) * TAPS
            pieces.append(turned[:, at : at + TAPS])
        banded(pieces, tb, s)

    def finish(pre, slots):
        for side in range(2):
            gvn[:, slots[side] - 1] = pre[side].reshape(CH, ROWS, COLS).astype(jnp.bfloat16)

    inner(gs, tb, pre_in)

    if comm:
        some, few = pl.ds(0, MEMBERS - 1), pl.ds(0, RING - 1)
        pltpu.make_async_copy(recv1.at[some], recv1.at[some], rrecv.at[0]).wait()
        red[...] = jnp.sum(recv1[...], axis=0) * scale
        for other, peer in ring:
            remote(red, recv2.at[peers.z], rsend.at[1], rrecv.at[1], peer).start()
        recv2[peers.z] = red[...]

        finish(pre_in, (2, 3))
        outer_own(gs, tb, pre_out)
        gup.wait()
        gdown.wait()
        for slot, keep in ((0, has_below), (PLANES + 1, has_above)):
            for row in range(ROWS):
                value = gs[slot, row + 1, CH : 2 * CH, :].astype(jnp.float32) * keep
                shifted(value, gs, slot, row, True)

        pltpu.make_async_copy(recv2.at[few], recv2.at[few], rrecv.at[1]).wait()
        final[...] = jnp.sum(recv2[...], axis=0)
        for other, peer in group:
            remote(final, res.at[mine], rsend.at[2], rrecv.at[2], peer).start()
        res[mine] = final[...]
    else:
        finish(pre_in, (2, 3))
        outer_own(gs, tb, pre_out)
        res[...] = pay[...] * scale

    outer_halo(gs, tb, pre_out, 0)
    outer_halo(gs, tb, pre_out, 1)
    finish(pre_out, (1, 4))
    if comm:
        up_copy.wait_send()
        down_copy.wait_send()
        pltpu.make_async_copy(recv1.at[some], recv1.at[some], rsend.at[0]).wait()
        pltpu.make_async_copy(recv2.at[few], recv2.at[few], rsend.at[1]).wait()
        pltpu.make_async_copy(recv1.at[some], recv1.at[some], rsend.at[2]).wait()
        pltpu.make_async_copy(recv1.at[some], recv1.at[some], rrecv.at[2]).wait()


def write_out(act_in, gvol_in, res, act, gvol, gk, go, gk_ref, go_ref, sem):
    pairs = ((act_in, act), (gvol_in, gvol), (gk_ref, gk), (go_ref, go))
    copies = [pltpu.make_async_copy(src, dst, sem.at[i]) for i, (src, dst) in enumerate(pairs)]
    copies[0].start()
    copies[1].start()
    unpack(res[:CHUNKS].reshape(PACKED, COLS), gk_ref)
    copies[2].start()
    biases = res[CHUNKS : CHUNKS + 4].reshape(CH, COLS)
    go_ref[...] = biases.T[2 * CH : 2 * CH + 1, :]
    copies[3].start()
    for copy in copies:
        copy.wait()


def layer(comm, scale, volume, kernel, offset, upstream):
    taps = jnp.transpose(kernel, (2, 3, 4, 0, 1)).reshape(27 * CH, CH)
    shape = (CH, PLANES, ROWS, COLS)
    wide = (PLANES + 2, ROWS + 2, TAPS, COLS)
    half, full = jnp.bfloat16, jnp.float32
    hbm = pl.BlockSpec(memory_space=pltpu.HBM)
    vmem = pl.BlockSpec(memory_space=pltpu.VMEM)
    act, gvol, res = pl.pallas_call(
        functools.partial(body, comm, scale),
        out_shape=(
            pltpu.VMEM(shape, half),
            pltpu.VMEM(shape, half),
            pltpu.VMEM((MEMBERS, 8, COLS), full),
        ),
        in_specs=[hbm, hbm, hbm, hbm],
        out_specs=(vmem, vmem, vmem),
        scratch_shapes=[
            pltpu.VMEM((27 * CH, CH), half),
            pltpu.SMEM((CH,), full),
            pltpu.VMEM(shape, half),
            pltpu.VMEM((2, CH, ROWS, COLS), half),
            pltpu.VMEM(shape, half),
            pltpu.VMEM((PLANES + 2, CH * ROWS, COLS), full),
            pltpu.VMEM(wide, half),
            pltpu.VMEM(wide, half),
            pltpu.VMEM((BLOCK * CH, 3 * DEEP), half),
            pltpu.VMEM((BLOCK * CH, 3 * DEEP), half),
            pltpu.VMEM((2, CH * ROWS, COLS), full),
            pltpu.VMEM((2, CH * ROWS, COLS), full),
            pltpu.VMEM((4 * TAPS, 2 * COLS), full),
            pltpu.VMEM((MEMBERS, 8, COLS), full),
            pltpu.VMEM((MEMBERS, 8, COLS), full),
            pltpu.VMEM((8, COLS), full),
            pltpu.VMEM((RING, 8, COLS), full),
            pltpu.VMEM((8, COLS), full),
            pltpu.SemaphoreType.DMA((7,)),
            pltpu.SemaphoreType.DMA((2,)),
            pltpu.SemaphoreType.DMA((2,)),
            pltpu.SemaphoreType.DMA((2,)),
            pltpu.SemaphoreType.DMA((2,)),
            pltpu.SemaphoreType.DMA((3,)),
            pltpu.SemaphoreType.DMA((3,)),
            pltpu.SemaphoreType.REGULAR((6,)),
        ],
        compiler_params=pltpu.CompilerParams(
            vmem_limit_bytes=VMEM,
            **({"collective_id": 0, "has_side_effects": True} if comm else {}),
        ),
        cost_estimate=pl.CostEstimate(flops=10**10, bytes_accessed=4 * 10**6, transcendentals=10**6),
    )(volume.reshape(shape), taps, offset, upstream.reshape(shape))
    act, gvol, gk, go = pl.pallas_call(
        write_out,
        out_shape=(
            jax.ShapeDtypeStruct(shape, half),
            jax.ShapeDtypeStruct(shape, half),
            jax.ShapeDtypeStruct((27 * CH, CH), full),
            jax.ShapeDtypeStruct((1, CH), full),
        ),
        in_specs=[vmem, vmem, vmem],
        out_specs=(hbm, hbm, hbm, hbm),
        scratch_shapes=[
            pltpu.VMEM((27 * CH, CH), full),
            pltpu.VMEM((1, CH), full),
            pltpu.SemaphoreType.DMA((4,)),
        ],
        compiler_params=pltpu.CompilerParams(vmem_limit_bytes=8 * 1024 * 1024),
        cost_estimate=pl.CostEstimate(flops=10**5, bytes_accessed=3 * 10**6, transcendentals=0),
    )(act, gvol, res)
    return (
        act.reshape(volume.shape),
        gvol.reshape(volume.shape),
        jnp.transpose(gk.reshape(3, 3, 3, CH, CH), (3, 4, 0, 1, 2)),
        go.reshape(CH),
    )


def solution(mesh):
    cells = mesh.shape["batch"] * mesh.shape["slab"] * PLANES * ROWS * COLS
    split = P("batch", None, "slab", None, None)
    return jax.shard_map(
        functools.partial(layer, True, cells**-0.5),
        mesh=mesh,
        in_specs=(split, P(), P(), split),
        out_specs=(split, split, P(), P()),
        check_vma=False,
    )
```

```python
import functools

import jax
import jax.numpy as jnp
from jax import lax
from jax.experimental import pallas as pl
from jax.experimental.pallas import tpu as pltpu
from jax.sharding import PartitionSpec as P

MESH = pl.DeviceIdType.MESH
VMEM = 65_500_000
CH = 32
PLANES = 4
ROWS = 16
COLS = 128
BLOCK = 8
WIN = BLOCK + 2
TAPS = 3 * CH
DEEP = 1024
GROUPS = 4
RING = 8
MEMBERS = 8 * GROUPS
PACKED = 27 * CH // 4
CHUNKS = PACKED // 8


def banded(pieces, out_ref, plane):
    whole = jnp.concatenate(pieces, axis=1)
    for row in range(BLOCK):
        parts = [whole]
        if row > 0:
            parts.insert(0, jnp.zeros((CH, row * TAPS), jnp.float32))
        parts.append(jnp.zeros((CH, DEEP - (row + 3) * TAPS), jnp.float32))
        block = jnp.concatenate(parts, axis=1)
        out_ref[row * CH : (row + 1) * CH, plane * DEEP : (plane + 1) * DEEP] = block.astype(
            jnp.bfloat16
        )


def shifted(values, out_ref, slot, row, flip):
    lane = lax.broadcasted_iota(jnp.int32, (CH, COLS), 1)
    left = jnp.where(lane == 0, 0.0, pltpu.roll(values, 1, 1))
    right = jnp.where(lane == COLS - 1, 0.0, pltpu.roll(values, COLS - 1, 1))
    if flip:
        left, right = right, left
    out_ref[slot, row + 1, 0:CH, :] = left.astype(jnp.bfloat16)
    out_ref[slot, row + 1, CH : 2 * CH, :] = values.astype(jnp.bfloat16)
    out_ref[slot, row + 1, 2 * CH : 3 * CH, :] = right.astype(jnp.bfloat16)


def clear_edges(ref):
    zero = jnp.zeros((TAPS, COLS), jnp.bfloat16)
    for slot in range(PLANES + 2):
        ref[slot, 0] = zero
        ref[slot, ROWS + 1] = zero


def window(ref, slot, half):
    rows = ref[slot, half * BLOCK : half * BLOCK + WIN].reshape(WIN * TAPS, COLS)
    return jnp.concatenate([rows, jnp.zeros((DEEP - WIN * TAPS, COLS), jnp.bfloat16)], axis=0)


def product(src_ref, t_ref, first, slots, half):
    sides = [jnp.concatenate([window(src_ref, s, half) for s in group], axis=0) for group in slots]
    columns = slice(first * DEEP, (first + len(slots[0])) * DEEP)
    rhs = jnp.concatenate(sides, axis=1)
    return jnp.dot(t_ref[:, columns], rhs, preferred_element_type=jnp.float32)


def put(out_ref, side, half, value, add):
    for row in range(BLOCK):
        at = pl.ds(half * BLOCK + row, CH, stride=ROWS)
        part = value[row * CH : (row + 1) * CH]
        out_ref[side, at, :] = part + out_ref[side, at, :] if add else part


def inner(src_ref, t_ref, out_ref):
    for half in range(ROWS // BLOCK):
        acc = product(src_ref, t_ref, 0, [(1, 2, 3), (2, 3, 4)], half)
        put(out_ref, 0, half, acc[:, :COLS], False)
        put(out_ref, 1, half, acc[:, COLS:], False)


def outer_own(src_ref, t_ref, out_ref):
    for half in range(ROWS // BLOCK):
        both = product(src_ref, t_ref, 1, [(1,), (PLANES,)], half)
        low = both[:, :COLS] + product(src_ref, t_ref, 2, [(2,)], half)
        high = both[:, COLS:] + product(src_ref, t_ref, 0, [(PLANES - 1,)], half)
        put(out_ref, 0, half, low, False)
        put(out_ref, 1, half, high, False)


def outer_halo(src_ref, t_ref, out_ref, side):
    first, slot = (0, 0) if side == 0 else (2, PLANES + 1)
    for half in range(ROWS // BLOCK):
        put(out_ref, side, half, product(src_ref, t_ref, first, [(slot,)], half), True)


def weight_terms(gs_ref, xs_ref, pair, dacc_ref, first):
    lhs, rhs = [], []
    pad = jnp.ones((CH * 2, COLS), jnp.bfloat16)
    for row in range(0, ROWS, 2):
        for slot in pair:
            lhs.append(gs_ref[slot, row : row + 4].reshape(4 * TAPS, COLS))
            sides = [
                xs_ref[slot + s - 1, row + 1 : row + 3, CH : 2 * CH, :].reshape(2 * CH, COLS)
                for s in range(3)
            ]
            rhs.append(jnp.concatenate(sides + [pad], axis=0))
    prod = lax.dot_general(
        jnp.concatenate(lhs, axis=1),
        jnp.concatenate(rhs, axis=1),
        (((1,), (1,)), ((), ())),
        preferred_element_type=jnp.float32,
    )
    if first:
        dacc_ref[...] = prod
    else:
        dacc_ref[...] += prod


def pack(total):
    block = lax.broadcasted_iota(jnp.int32, (TAPS, COLS), 1) // CH
    sides = []
    for side in range(2):
        rows = []
        for kh in range(3):
            even = total[(2 - kh) * TAPS : (3 - kh) * TAPS, side * COLS : (side + 1) * COLS]
            odd = total[(3 - kh) * TAPS : (4 - kh) * TAPS, side * COLS : (side + 1) * COLS]
            rows.append(jnp.where(block % 2 == 0, even, odd))
        value = jnp.concatenate(rows, axis=0)
        sides.append(value + pltpu.roll(value, CH, 1))
    block = lax.broadcasted_iota(jnp.int32, (3 * TAPS, COLS), 1) // CH
    value = jnp.where(block == 0, pltpu.roll(sides[1], 3 * CH, 1), sides[0])
    rest = value[PACKED:]
    moved = [pltpu.roll(rest, shift * CH, 1) for shift in (1, 3, 2)]
    return jnp.where(block[:PACKED] == 2, jnp.concatenate(moved, axis=0), value[:PACKED])


def unpack(full, out_ref):
    rest = pltpu.roll(full, 2 * CH, 1)[:, :CH]
    for s, shift in enumerate((3, 1, 0)):
        at = s * 3 * TAPS
        value = full if shift == 0 else pltpu.roll(full, shift * CH, 1)
        out_ref[at : at + PACKED, :] = value[:, :CH]
        few = 3 * TAPS - PACKED
        out_ref[at + PACKED : at + 3 * TAPS, :] = rest[s * few : (s + 1) * few]


class Peers:
    def __init__(self):
        self.batch, self.slab = lax.axis_index("batch"), lax.axis_index("slab")
        self.y, self.z = self.slab // RING, self.slab % RING
        x, core = self.batch // 2, self.batch % 2
        self.mine = self.batch * GROUPS + self.y
        xs = [wrapped(x + d, 4) for d in range(4)]
        cores = [core, 1 - core]
        ys = [wrapped(self.y + d, GROUPS) for d in range(GROUPS)]
        zs = [wrapped(self.z + d, RING) for d in range(RING)]
        group = [(dx, dy, dc) for dx in range(4) for dy in range(GROUPS) for dc in range(2)]
        group = sorted(group[1:], key=lambda t: -(min(t[0], 4 - t[0]) + min(t[1], GROUPS - t[1])))
        self.group = []
        for dx, dy, dc in group:
            batch = xs[dx] * 2 + cores[dc]
            self.group.append((batch * GROUPS + ys[dy], (batch, ys[dy] * RING + self.z)))
        ring = sorted(range(1, RING), key=lambda d: -min(d, RING - d))
        self.ring = [(zs[d], (self.batch, self.y * RING + zs[d])) for d in ring]

        def place(dx=0, dy=0, dz=0, dc=0):
            return (xs[dx] * 2 + cores[dc], ys[dy] * RING + zs[dz])

        self.x_near = [place(dx=1), place(dx=3)]
        self.x_all = [place(dx=1), place(dx=3), place(dx=2)]
        self.y_near = [place(dy=1), place(dy=GROUPS - 1)]
        self.z_near = [place(dz=1), place(dz=RING - 1)]
        self.z_next = [place(dz=2), place(dz=RING - 2)]
        self.twin = place(dc=1)
        self.above = (self.batch, wrapped(self.slab + 1, GROUPS * RING))
        self.below = (self.batch, wrapped(self.slab + GROUPS * RING - 1, GROUPS * RING))


def wrapped(value, count):
    return jnp.where(value >= count, value - count, value)


def remote(src, dst, send, recv, peer):
    return pltpu.make_async_remote_copy(src, dst, send, recv, peer, MESH)


def tell(sem, peers):
    for peer in peers:
        pl.semaphore_signal(sem, 1, device_id=peer, device_id_type=MESH)


def body(
    comm,
    scale,
    vol,
    w_hbm,
    off_hbm,
    up,
    actn,
    gvn,
    res,
    w_ref,
    off_ref,
    vown,
    vhalo,
    upn,
    xf,
    xs,
    gs,
    tf,
    tb,
    pre_in,
    pre_out,
    dacc,
    pay,
    recv1,
    red,
    recv2,
    final,
    local_sem,
    vsend,
    vrecv,
    gsend,
    grecv,
    rsend,
    rrecv,
    known,
):
    if comm:
        peers = Peers()
        group, ring = peers.group, peers.ring
        barrier = pltpu.get_barrier_semaphore()
        near = [peers.above, peers.below] + peers.z_near + peers.y_near + peers.x_near
        near.append(peers.twin)
        tell(barrier, near)

    inside = pl.ds(1, PLANES - 2)
    load_top = pltpu.make_async_copy(vol.at[:, PLANES - 1], vown.at[:, PLANES - 1], local_sem.at[2])
    load_top.start()
    load_low = pltpu.make_async_copy(vol.at[:, 0], vown.at[:, 0], local_sem.at[3])
    load_low.start()
    load_w = pltpu.make_async_copy(w_hbm, w_ref, local_sem.at[4])
    load_w.start()
    load_v = pltpu.make_async_copy(vol.at[:, inside], vown.at[:, inside], local_sem.at[0])
    load_v.start()
    load_o = pltpu.make_async_copy(off_hbm, off_ref, local_sem.at[5])
    load_o.start()
    load_u = pltpu.make_async_copy(up, upn, local_sem.at[1])
    load_u.start()
    clear_edges(xs)
    clear_edges(gs)

    if comm:
        pl.semaphore_wait(barrier, len(near))
        load_top.wait()
        load_low.wait()
        up_copy = remote(vown.at[:, PLANES - 1], vhalo.at[0], vsend.at[0], vrecv.at[0], peers.above)
        down_copy = remote(vown.at[:, 0], vhalo.at[1], vsend.at[1], vrecv.at[1], peers.below)
        up_copy.start()
        down_copy.start()
        tell(known.at[0], peers.y_near)
        tell(known.at[1], peers.x_near)
        tell(known.at[2], peers.z_near)
        has_below = jnp.where(peers.slab == 0, 0.0, 1.0)
        has_above = jnp.where(peers.slab == GROUPS * RING - 1, 0.0, 1.0)
    else:
        load_top.wait()
        load_low.wait()

    load_w.wait()
    taps = w_ref[...].astype(jnp.float32)

    def tap(s, u, k):
        at = ((s * 3 + u) * 3 + k) * CH
        return taps[at : at + CH]

    for s in range(3):
        pieces = [jnp.concatenate([tap(s, u, k) for k in range(3)], axis=1) for u in range(3)]
        banded(pieces, tf, s)

    def spread_volume(slot, values):
        xf[slot] = values.astype(jnp.float32).reshape(CH * ROWS, COLS)
        for row in range(ROWS):
            shifted(xf[slot, pl.ds(row, CH, stride=ROWS), :], xs, slot, row, False)

    load_v.wait()
    for plane in range(PLANES):
        spread_volume(plane + 1, vown[:, plane])
    load_o.wait()
    load_u.wait()

    def activate(pre, slots, sides):
        for side in sides:
            plane = slots[side] - 1
            for ch in range(CH):
                at = pl.ds(ch * ROWS, ROWS)
                value = pre[side, at, :] + off_ref[ch]
                sig = 0.5 * jnp.tanh(0.5 * value) + 0.5
                actn[ch, plane] = (value * sig).astype(jnp.bfloat16)
                grad = upn[ch, plane].astype(jnp.float32) * sig * (1.0 + value * (1.0 - sig))
                pre[side, at, :] = grad
            for row in range(ROWS):
                shifted(pre[side, pl.ds(row, CH, stride=ROWS), :], gs, plane + 1, row, True)

    inner(xs, tf, pre_in)
    if comm:
        for i in range(3):
            pl.semaphore_wait(known.at[i], 2)
        tell(known.at[3], peers.x_all)
        tell(known.at[4], peers.z_next)
    activate(pre_in, (2, 3), (0, 1))
    weight_terms(gs, xs, (2, 3), dacc, True)
    outer_own(xs, tf, pre_out)
    if comm:
        pl.semaphore_wait(known.at[3], 3)
        pl.semaphore_wait(known.at[4], 2)
        tell(known.at[5], [peers.twin])

    if comm:

        def edge(slot):
            return gs.at[slot, 1 : ROWS + 1, CH : 2 * CH, :]

        gup = remote(edge(PLANES), edge(0), gsend.at[0], grecv.at[0], peers.above)
        gdown = remote(edge(1), edge(PLANES + 1), gsend.at[1], grecv.at[1], peers.below)
        up_copy.wait_recv()
        spread_volume(0, vhalo[0].astype(jnp.float32) * has_below)
    else:
        for ref in (xs, gs):
            for slot in (0, PLANES + 1):
                ref[slot] = jnp.zeros_like(ref[slot])
    outer_halo(xs, tf, pre_out, 0)
    activate(pre_out, (1, 4), (0,))
    if comm:
        gdown.start()
        down_copy.wait_recv()
        spread_volume(PLANES + 1, vhalo[1].astype(jnp.float32) * has_above)
    outer_halo(xs, tf, pre_out, 1)
    activate(pre_out, (1, 4), (1,))
    if comm:
        gup.start()
    weight_terms(gs, xs, (1, 4), dacc, False)

    packed = pack(dacc[...])
    pay[:CHUNKS] = packed.reshape(CHUNKS, 8, COLS)
    sums = [dacc[row * TAPS + CH : row * TAPS + 2 * CH, COLS:] for row in (1, 2)]
    pay[CHUNKS : CHUNKS + 4] = (sums[0] + sums[1]).reshape(4, 8, COLS)
    pay[CHUNKS + 4 :] = jnp.zeros((MEMBERS - CHUNKS - 4, 8, COLS), jnp.float32)

    if comm:
        pl.semaphore_wait(known.at[5], 1)
        mine = peers.mine
        for other, peer in group:
            remote(pay.at[other], recv1.at[mine], rsend.at[0], rrecv.at[0], peer).start()
        recv1[mine] = pay[mine]

    turned = taps.T
    for s in range(3):
        pieces = []
        for u in range(3):
            at = ((2 - s) * 3 + 2 - u) * TAPS
            pieces.append(turned[:, at : at + TAPS])
        banded(pieces, tb, s)

    def finish(pre, slots):
        for side in range(2):
            gvn[:, slots[side] - 1] = pre[side].reshape(CH, ROWS, COLS).astype(jnp.bfloat16)

    inner(gs, tb, pre_in)

    if comm:
        some, few = pl.ds(0, MEMBERS - 1), pl.ds(0, RING - 1)
        pltpu.make_async_copy(recv1.at[some], recv1.at[some], rrecv.at[0]).wait()
        red[...] = jnp.sum(recv1[...], axis=0) * scale
        for other, peer in ring:
            remote(red, recv2.at[peers.z], rsend.at[1], rrecv.at[1], peer).start()
        recv2[peers.z] = red[...]

        finish(pre_in, (2, 3))
        outer_own(gs, tb, pre_out)
        gup.wait()
        gdown.wait()
        for slot, keep in ((0, has_below), (PLANES + 1, has_above)):
            for row in range(ROWS):
                value = gs[slot, row + 1, CH : 2 * CH, :].astype(jnp.float32) * keep
                shifted(value, gs, slot, row, True)

        pltpu.make_async_copy(recv2.at[few], recv2.at[few], rrecv.at[1]).wait()
        final[...] = jnp.sum(recv2[...], axis=0)
        for other, peer in group:
            remote(final, res.at[mine], rsend.at[2], rrecv.at[2], peer).start()
        res[mine] = final[...]
    else:
        finish(pre_in, (2, 3))
        outer_own(gs, tb, pre_out)
        res[...] = pay[...] * scale

    outer_halo(gs, tb, pre_out, 0)
    outer_halo(gs, tb, pre_out, 1)
    finish(pre_out, (1, 4))
    if comm:
        up_copy.wait_send()
        down_copy.wait_send()
        pltpu.make_async_copy(recv1.at[some], recv1.at[some], rsend.at[0]).wait()
        pltpu.make_async_copy(recv2.at[few], recv2.at[few], rsend.at[1]).wait()
        pltpu.make_async_copy(recv1.at[some], recv1.at[some], rsend.at[2]).wait()
        pltpu.make_async_copy(recv1.at[some], recv1.at[some], rrecv.at[2]).wait()


def write_out(act_in, gvol_in, res, act, gvol, gk, go, gk_ref, go_ref, sem):
    pairs = ((act_in, act), (gvol_in, gvol), (gk_ref, gk), (go_ref, go))
    copies = [pltpu.make_async_copy(src, dst, sem.at[i]) for i, (src, dst) in enumerate(pairs)]
    copies[0].start()
    copies[1].start()
    unpack(res[:CHUNKS].reshape(PACKED, COLS), gk_ref)
    copies[2].start()
    biases = res[CHUNKS : CHUNKS + 4].reshape(CH, COLS)
    go_ref[...] = biases.T[2 * CH : 2 * CH + 1, :]
    copies[3].start()
    for copy in copies:
        copy.wait()


def layer(comm, scale, volume, kernel, offset, upstream):
    taps = jnp.transpose(kernel, (2, 3, 4, 0, 1)).reshape(27 * CH, CH)
    shape = (CH, PLANES, ROWS, COLS)
    wide = (PLANES + 2, ROWS + 2, TAPS, COLS)
    half, full = jnp.bfloat16, jnp.float32
    hbm = pl.BlockSpec(memory_space=pltpu.HBM)
    vmem = pl.BlockSpec(memory_space=pltpu.VMEM)
    act, gvol, res = pl.pallas_call(
        functools.partial(body, comm, scale),
        out_shape=(
            pltpu.VMEM(shape, half),
            pltpu.VMEM(shape, half),
            pltpu.VMEM((MEMBERS, 8, COLS), full),
        ),
        in_specs=[hbm, hbm, hbm, hbm],
        out_specs=(vmem, vmem, vmem),
        scratch_shapes=[
            pltpu.VMEM((27 * CH, CH), half),
            pltpu.SMEM((CH,), full),
            pltpu.VMEM(shape, half),
            pltpu.VMEM((2, CH, ROWS, COLS), half),
            pltpu.VMEM(shape, half),
            pltpu.VMEM((PLANES + 2, CH * ROWS, COLS), full),
            pltpu.VMEM(wide, half),
            pltpu.VMEM(wide, half),
            pltpu.VMEM((BLOCK * CH, 3 * DEEP), half),
            pltpu.VMEM((BLOCK * CH, 3 * DEEP), half),
            pltpu.VMEM((2, CH * ROWS, COLS), full),
            pltpu.VMEM((2, CH * ROWS, COLS), full),
            pltpu.VMEM((4 * TAPS, 2 * COLS), full),
            pltpu.VMEM((MEMBERS, 8, COLS), full),
            pltpu.VMEM((MEMBERS, 8, COLS), full),
            pltpu.VMEM((8, COLS), full),
            pltpu.VMEM((RING, 8, COLS), full),
            pltpu.VMEM((8, COLS), full),
            pltpu.SemaphoreType.DMA((7,)),
            pltpu.SemaphoreType.DMA((2,)),
            pltpu.SemaphoreType.DMA((2,)),
            pltpu.SemaphoreType.DMA((2,)),
            pltpu.SemaphoreType.DMA((2,)),
            pltpu.SemaphoreType.DMA((3,)),
            pltpu.SemaphoreType.DMA((3,)),
            pltpu.SemaphoreType.REGULAR((6,)),
        ],
        compiler_params=pltpu.CompilerParams(
            vmem_limit_bytes=VMEM,
            **({"collective_id": 0, "has_side_effects": True} if comm else {}),
        ),
        cost_estimate=pl.CostEstimate(flops=10**10, bytes_accessed=4 * 10**6, transcendentals=10**6),
    )(volume.reshape(shape), taps, offset, upstream.reshape(shape))
    act, gvol, gk, go = pl.pallas_call(
        write_out,
        out_shape=(
            jax.ShapeDtypeStruct(shape, half),
            jax.ShapeDtypeStruct(shape, half),
            jax.ShapeDtypeStruct((27 * CH, CH), full),
            jax.ShapeDtypeStruct((1, CH), full),
        ),
        in_specs=[vmem, vmem, vmem],
        out_specs=(hbm, hbm, hbm, hbm),
        scratch_shapes=[
            pltpu.VMEM((27 * CH, CH), full),
            pltpu.VMEM((1, CH), full),
            pltpu.SemaphoreType.DMA((4,)),
        ],
        compiler_params=pltpu.CompilerParams(vmem_limit_bytes=8 * 1024 * 1024),
        cost_estimate=pl.CostEstimate(flops=10**5, bytes_accessed=3 * 10**6, transcendentals=0),
    )(act, gvol, res)
    return (
        act.reshape(volume.shape),
        gvol.reshape(volume.shape),
        jnp.transpose(gk.reshape(3, 3, 3, CH, CH), (3, 4, 0, 1, 2)),
        go.reshape(CH),
    )


def solution(mesh):
    cells = mesh.shape["batch"] * mesh.shape["slab"] * PLANES * ROWS * COLS
    split = P("batch", None, "slab", None, None)
    return jax.shard_map(
        functools.partial(layer, True, cells**-0.5),
        mesh=mesh,
        in_specs=(split, P(), P(), split),
        out_specs=(split, split, P(), P()),
        check_vma=False,
    )
```

```python
import functools

import jax
import jax.numpy as jnp
from jax import lax
from jax.experimental import pallas as pl
from jax.experimental.pallas import tpu as pltpu
from jax.sharding import PartitionSpec as P

MESH = pl.DeviceIdType.MESH
VMEM = 65_500_000
CH = 32
PLANES = 4
ROWS = 16
COLS = 128
BLOCK = 8
WIN = BLOCK + 2
TAPS = 3 * CH
DEEP = 1024
GROUPS = 4
RING = 8
MEMBERS = 8 * GROUPS
PACKED = 27 * CH // 4
CHUNKS = PACKED // 8


def banded(pieces, out_ref, plane):
    whole = jnp.concatenate(pieces, axis=1)
    for row in range(BLOCK):
        parts = [whole]
        if row > 0:
            parts.insert(0, jnp.zeros((CH, row * TAPS), jnp.float32))
        parts.append(jnp.zeros((CH, DEEP - (row + 3) * TAPS), jnp.float32))
        block = jnp.concatenate(parts, axis=1)
        out_ref[row * CH : (row + 1) * CH, plane * DEEP : (plane + 1) * DEEP] = block.astype(
            jnp.bfloat16
        )


def shifted(values, out_ref, slot, row, flip):
    lane = lax.broadcasted_iota(jnp.int32, (CH, COLS), 1)
    left = jnp.where(lane == 0, 0.0, pltpu.roll(values, 1, 1))
    right = jnp.where(lane == COLS - 1, 0.0, pltpu.roll(values, COLS - 1, 1))
    if flip:
        left, right = right, left
    out_ref[slot, row + 1, 0:CH, :] = left.astype(jnp.bfloat16)
    out_ref[slot, row + 1, CH : 2 * CH, :] = values.astype(jnp.bfloat16)
    out_ref[slot, row + 1, 2 * CH : 3 * CH, :] = right.astype(jnp.bfloat16)


def clear_edges(ref):
    zero = jnp.zeros((TAPS, COLS), jnp.bfloat16)
    for slot in range(PLANES + 2):
        ref[slot, 0] = zero
        ref[slot, ROWS + 1] = zero


def window(ref, slot, half):
    rows = ref[slot, half * BLOCK : half * BLOCK + WIN].reshape(WIN * TAPS, COLS)
    return jnp.concatenate([rows, jnp.zeros((DEEP - WIN * TAPS, COLS), jnp.bfloat16)], axis=0)


def product(src_ref, t_ref, first, slots, half):
    sides = [jnp.concatenate([window(src_ref, s, half) for s in group], axis=0) for group in slots]
    columns = slice(first * DEEP, (first + len(slots[0])) * DEEP)
    rhs = jnp.concatenate(sides, axis=1)
    return jnp.dot(t_ref[:, columns], rhs, preferred_element_type=jnp.float32)


def put(out_ref, side, half, value, add):
    for row in range(BLOCK):
        at = pl.ds(half * BLOCK + row, CH, stride=ROWS)
        part = value[row * CH : (row + 1) * CH]
        out_ref[side, at, :] = part + out_ref[side, at, :] if add else part


def inner(src_ref, t_ref, out_ref):
    for half in range(ROWS // BLOCK):
        acc = product(src_ref, t_ref, 0, [(1, 2, 3), (2, 3, 4)], half)
        put(out_ref, 0, half, acc[:, :COLS], False)
        put(out_ref, 1, half, acc[:, COLS:], False)


def outer_own(src_ref, t_ref, out_ref):
    for half in range(ROWS // BLOCK):
        both = product(src_ref, t_ref, 1, [(1,), (PLANES,)], half)
        low = both[:, :COLS] + product(src_ref, t_ref, 2, [(2,)], half)
        high = both[:, COLS:] + product(src_ref, t_ref, 0, [(PLANES - 1,)], half)
        put(out_ref, 0, half, low, False)
        put(out_ref, 1, half, high, False)


def outer_halo(src_ref, t_ref, out_ref, side):
    first, slot = (0, 0) if side == 0 else (2, PLANES + 1)
    for half in range(ROWS // BLOCK):
        put(out_ref, side, half, product(src_ref, t_ref, first, [(slot,)], half), True)


def weight_terms(gs_ref, xs_ref, pair, dacc_ref, first):
    lhs, rhs = [], []
    pad = jnp.ones((CH * 2, COLS), jnp.bfloat16)
    for row in range(0, ROWS, 2):
        for slot in pair:
            lhs.append(gs_ref[slot, row : row + 4].reshape(4 * TAPS, COLS))
            sides = [
                xs_ref[slot + s - 1, row + 1 : row + 3, CH : 2 * CH, :].reshape(2 * CH, COLS)
                for s in range(3)
            ]
            rhs.append(jnp.concatenate(sides + [pad], axis=0))
    prod = lax.dot_general(
        jnp.concatenate(lhs, axis=1),
        jnp.concatenate(rhs, axis=1),
        (((1,), (1,)), ((), ())),
        preferred_element_type=jnp.float32,
    )
    if first:
        dacc_ref[...] = prod
    else:
        dacc_ref[...] += prod


def pack(total):
    block = lax.broadcasted_iota(jnp.int32, (TAPS, COLS), 1) // CH
    sides = []
    for side in range(2):
        rows = []
        for kh in range(3):
            even = total[(2 - kh) * TAPS : (3 - kh) * TAPS, side * COLS : (side + 1) * COLS]
            odd = total[(3 - kh) * TAPS : (4 - kh) * TAPS, side * COLS : (side + 1) * COLS]
            rows.append(jnp.where(block % 2 == 0, even, odd))
        value = jnp.concatenate(rows, axis=0)
        sides.append(value + pltpu.roll(value, CH, 1))
    block = lax.broadcasted_iota(jnp.int32, (3 * TAPS, COLS), 1) // CH
    value = jnp.where(block == 0, pltpu.roll(sides[1], 3 * CH, 1), sides[0])
    rest = value[PACKED:]
    moved = [pltpu.roll(rest, shift * CH, 1) for shift in (1, 3, 2)]
    return jnp.where(block[:PACKED] == 2, jnp.concatenate(moved, axis=0), value[:PACKED])


def unpack(full, out_ref):
    rest = pltpu.roll(full, 2 * CH, 1)[:, :CH]
    for s, shift in enumerate((3, 1, 0)):
        at = s * 3 * TAPS
        value = full if shift == 0 else pltpu.roll(full, shift * CH, 1)
        out_ref[at : at + PACKED, :] = value[:, :CH]
        few = 3 * TAPS - PACKED
        out_ref[at + PACKED : at + 3 * TAPS, :] = rest[s * few : (s + 1) * few]


class Peers:
    def __init__(self):
        self.batch, self.slab = lax.axis_index("batch"), lax.axis_index("slab")
        self.y, self.z = self.slab // RING, self.slab % RING
        x, core = self.batch // 2, self.batch % 2
        self.mine = self.batch * GROUPS + self.y
        xs = [wrapped(x + d, 4) for d in range(4)]
        cores = [core, 1 - core]
        ys = [wrapped(self.y + d, GROUPS) for d in range(GROUPS)]
        zs = [wrapped(self.z + d, RING) for d in range(RING)]
        group = [(dx, dy, dc) for dx in range(4) for dy in range(GROUPS) for dc in range(2)]
        group = sorted(group[1:], key=lambda t: -(min(t[0], 4 - t[0]) + min(t[1], GROUPS - t[1])))
        self.group = []
        for dx, dy, dc in group:
            batch = xs[dx] * 2 + cores[dc]
            self.group.append((batch * GROUPS + ys[dy], (batch, ys[dy] * RING + self.z)))
        ring = sorted(range(1, RING), key=lambda d: -min(d, RING - d))
        self.ring = [(zs[d], (self.batch, self.y * RING + zs[d])) for d in ring]

        def place(dx=0, dy=0, dz=0, dc=0):
            return (xs[dx] * 2 + cores[dc], ys[dy] * RING + zs[dz])

        self.x_near = [place(dx=1), place(dx=3)]
        self.x_all = [place(dx=1), place(dx=3), place(dx=2)]
        self.y_near = [place(dy=1), place(dy=GROUPS - 1)]
        self.z_near = [place(dz=1), place(dz=RING - 1)]
        self.z_next = [place(dz=2), place(dz=RING - 2)]
        self.twin = place(dc=1)
        self.above = (self.batch, wrapped(self.slab + 1, GROUPS * RING))
        self.below = (self.batch, wrapped(self.slab + GROUPS * RING - 1, GROUPS * RING))


def wrapped(value, count):
    return jnp.where(value >= count, value - count, value)


def remote(src, dst, send, recv, peer):
    return pltpu.make_async_remote_copy(src, dst, send, recv, peer, MESH)


def tell(sem, peers):
    for peer in peers:
        pl.semaphore_signal(sem, 1, device_id=peer, device_id_type=MESH)


def body(
    comm,
    scale,
    vol,
    w_hbm,
    off_hbm,
    up,
    actn,
    gvn,
    res,
    w_ref,
    off_ref,
    vown,
    vhalo,
    upn,
    xf,
    xs,
    gs,
    tf,
    tb,
    pre_in,
    pre_out,
    dacc,
    pay,
    recv1,
    red,
    recv2,
    final,
    local_sem,
    vsend,
    vrecv,
    gsend,
    grecv,
    rsend,
    rrecv,
    known,
):
    load_top = pltpu.make_async_copy(vol.at[:, PLANES - 1], vown.at[:, PLANES - 1], local_sem.at[2])
    load_top.start()
    load_low = pltpu.make_async_copy(vol.at[:, 0], vown.at[:, 0], local_sem.at[3])
    load_low.start()

    if comm:
        peers = Peers()
        group, ring = peers.group, peers.ring
        barrier = pltpu.get_barrier_semaphore()
        near = [peers.above, peers.below] + peers.z_near + peers.y_near + peers.x_near
        near.append(peers.twin)
        tell(barrier, near)

    inside = pl.ds(1, PLANES - 2)
    load_w = pltpu.make_async_copy(w_hbm, w_ref, local_sem.at[4])
    load_w.start()
    load_v = pltpu.make_async_copy(vol.at[:, inside], vown.at[:, inside], local_sem.at[0])
    load_v.start()
    load_o = pltpu.make_async_copy(off_hbm, off_ref, local_sem.at[5])
    load_o.start()
    load_u = pltpu.make_async_copy(up, upn, local_sem.at[1])
    load_u.start()

    if comm:
        pl.semaphore_wait(barrier, len(near))
        load_top.wait()
        load_low.wait()
        up_copy = remote(vown.at[:, PLANES - 1], vhalo.at[0], vsend.at[0], vrecv.at[0], peers.above)
        down_copy = remote(vown.at[:, 0], vhalo.at[1], vsend.at[1], vrecv.at[1], peers.below)
        up_copy.start()
        down_copy.start()
        tell(known.at[0], peers.y_near)
        tell(known.at[1], peers.x_near)
        tell(known.at[2], peers.z_near)
        has_below = jnp.where(peers.slab == 0, 0.0, 1.0)
        has_above = jnp.where(peers.slab == GROUPS * RING - 1, 0.0, 1.0)
    else:
        load_top.wait()
        load_low.wait()

    clear_edges(xs)
    clear_edges(gs)
    load_w.wait()
    taps = w_ref[...].astype(jnp.float32)

    def tap(s, u, k):
        at = ((s * 3 + u) * 3 + k) * CH
        return taps[at : at + CH]

    for s in range(3):
        pieces = [jnp.concatenate([tap(s, u, k) for k in range(3)], axis=1) for u in range(3)]
        banded(pieces, tf, s)

    def spread_volume(slot, values):
        xf[slot] = values.astype(jnp.float32).reshape(CH * ROWS, COLS)
        for row in range(ROWS):
            shifted(xf[slot, pl.ds(row, CH, stride=ROWS), :], xs, slot, row, False)

    load_v.wait()
    for plane in range(PLANES):
        spread_volume(plane + 1, vown[:, plane])
    load_o.wait()
    load_u.wait()

    def activate(pre, slots, sides):
        for side in sides:
            plane = slots[side] - 1
            for ch in range(CH):
                at = pl.ds(ch * ROWS, ROWS)
                value = pre[side, at, :] + off_ref[ch]
                sig = 0.5 * jnp.tanh(0.5 * value) + 0.5
                actn[ch, plane] = (value * sig).astype(jnp.bfloat16)
                grad = upn[ch, plane].astype(jnp.float32) * sig * (1.0 + value * (1.0 - sig))
                pre[side, at, :] = grad
            for row in range(ROWS):
                shifted(pre[side, pl.ds(row, CH, stride=ROWS), :], gs, plane + 1, row, True)

    inner(xs, tf, pre_in)
    if comm:
        for i in range(3):
            pl.semaphore_wait(known.at[i], 2)
        tell(known.at[3], peers.x_all)
        tell(known.at[4], peers.z_next)
    activate(pre_in, (2, 3), (0, 1))
    weight_terms(gs, xs, (2, 3), dacc, True)
    outer_own(xs, tf, pre_out)
    if comm:
        pl.semaphore_wait(known.at[3], 3)
        pl.semaphore_wait(known.at[4], 2)
        tell(known.at[5], [peers.twin])

    if comm:

        def edge(slot):
            return gs.at[slot, 1 : ROWS + 1, CH : 2 * CH, :]

        gup = remote(edge(PLANES), edge(0), gsend.at[0], grecv.at[0], peers.above)
        gdown = remote(edge(1), edge(PLANES + 1), gsend.at[1], grecv.at[1], peers.below)
        up_copy.wait_recv()
        spread_volume(0, vhalo[0].astype(jnp.float32) * has_below)
    else:
        for ref in (xs, gs):
            for slot in (0, PLANES + 1):
                ref[slot] = jnp.zeros_like(ref[slot])
    outer_halo(xs, tf, pre_out, 0)
    activate(pre_out, (1, 4), (0,))
    if comm:
        gdown.start()
        down_copy.wait_recv()
        spread_volume(PLANES + 1, vhalo[1].astype(jnp.float32) * has_above)
    outer_halo(xs, tf, pre_out, 1)
    activate(pre_out, (1, 4), (1,))
    if comm:
        gup.start()
    weight_terms(gs, xs, (1, 4), dacc, False)

    packed = pack(dacc[...])
    pay[:CHUNKS] = packed.reshape(CHUNKS, 8, COLS)
    sums = [dacc[row * TAPS + CH : row * TAPS + 2 * CH, COLS:] for row in (1, 2)]
    pay[CHUNKS : CHUNKS + 4] = (sums[0] + sums[1]).reshape(4, 8, COLS)
    pay[CHUNKS + 4 :] = jnp.zeros((MEMBERS - CHUNKS - 4, 8, COLS), jnp.float32)

    if comm:
        pl.semaphore_wait(known.at[5], 1)
        mine = peers.mine
        for other, peer in group:
            remote(pay.at[other], recv1.at[mine], rsend.at[0], rrecv.at[0], peer).start()
        recv1[mine] = pay[mine]

    turned = taps.T
    for s in range(3):
        pieces = []
        for u in range(3):
            at = ((2 - s) * 3 + 2 - u) * TAPS
            pieces.append(turned[:, at : at + TAPS])
        banded(pieces, tb, s)

    def finish(pre, slots):
        for side in range(2):
            gvn[:, slots[side] - 1] = pre[side].reshape(CH, ROWS, COLS).astype(jnp.bfloat16)

    inner(gs, tb, pre_in)

    if comm:
        some, few = pl.ds(0, MEMBERS - 1), pl.ds(0, RING - 1)
        pltpu.make_async_copy(recv1.at[some], recv1.at[some], rrecv.at[0]).wait()
        red[...] = jnp.sum(recv1[...], axis=0) * scale
        for other, peer in ring:
            remote(red, recv2.at[peers.z], rsend.at[1], rrecv.at[1], peer).start()
        recv2[peers.z] = red[...]

        finish(pre_in, (2, 3))
        outer_own(gs, tb, pre_out)
        gup.wait()
        gdown.wait()
        for slot, keep in ((0, has_below), (PLANES + 1, has_above)):
            for row in range(ROWS):
                value = gs[slot, row + 1, CH : 2 * CH, :].astype(jnp.float32) * keep
                shifted(value, gs, slot, row, True)

        pltpu.make_async_copy(recv2.at[few], recv2.at[few], rrecv.at[1]).wait()
        final[...] = jnp.sum(recv2[...], axis=0)
        for other, peer in group:
            remote(final, res.at[mine], rsend.at[2], rrecv.at[2], peer).start()
        res[mine] = final[...]
    else:
        finish(pre_in, (2, 3))
        outer_own(gs, tb, pre_out)
        res[...] = pay[...] * scale

    outer_halo(gs, tb, pre_out, 0)
    outer_halo(gs, tb, pre_out, 1)
    finish(pre_out, (1, 4))
    if comm:
        up_copy.wait_send()
        down_copy.wait_send()
        pltpu.make_async_copy(recv1.at[some], recv1.at[some], rsend.at[0]).wait()
        pltpu.make_async_copy(recv2.at[few], recv2.at[few], rsend.at[1]).wait()
        pltpu.make_async_copy(recv1.at[some], recv1.at[some], rsend.at[2]).wait()
        pltpu.make_async_copy(recv1.at[some], recv1.at[some], rrecv.at[2]).wait()


def write_out(act_in, gvol_in, res, act, gvol, gk, go, gk_ref, go_ref, sem):
    pairs = ((act_in, act), (gvol_in, gvol), (gk_ref, gk), (go_ref, go))
    copies = [pltpu.make_async_copy(src, dst, sem.at[i]) for i, (src, dst) in enumerate(pairs)]
    copies[0].start()
    copies[1].start()
    unpack(res[:CHUNKS].reshape(PACKED, COLS), gk_ref)
    copies[2].start()
    biases = res[CHUNKS : CHUNKS + 4].reshape(CH, COLS)
    go_ref[...] = biases.T[2 * CH : 2 * CH + 1, :]
    copies[3].start()
    for copy in copies:
        copy.wait()


def layer(comm, scale, volume, kernel, offset, upstream):
    taps = jnp.transpose(kernel, (2, 3, 4, 0, 1)).reshape(27 * CH, CH)
    shape = (CH, PLANES, ROWS, COLS)
    wide = (PLANES + 2, ROWS + 2, TAPS, COLS)
    half, full = jnp.bfloat16, jnp.float32
    hbm = pl.BlockSpec(memory_space=pltpu.HBM)
    vmem = pl.BlockSpec(memory_space=pltpu.VMEM)
    act, gvol, res = pl.pallas_call(
        functools.partial(body, comm, scale),
        out_shape=(
            pltpu.VMEM(shape, half),
            pltpu.VMEM(shape, half),
            pltpu.VMEM((MEMBERS, 8, COLS), full),
        ),
        in_specs=[hbm, hbm, hbm, hbm],
        out_specs=(vmem, vmem, vmem),
        scratch_shapes=[
            pltpu.VMEM((27 * CH, CH), half),
            pltpu.SMEM((CH,), full),
            pltpu.VMEM(shape, half),
            pltpu.VMEM((2, CH, ROWS, COLS), half),
            pltpu.VMEM(shape, half),
            pltpu.VMEM((PLANES + 2, CH * ROWS, COLS), full),
            pltpu.VMEM(wide, half),
            pltpu.VMEM(wide, half),
            pltpu.VMEM((BLOCK * CH, 3 * DEEP), half),
            pltpu.VMEM((BLOCK * CH, 3 * DEEP), half),
            pltpu.VMEM((2, CH * ROWS, COLS), full),
            pltpu.VMEM((2, CH * ROWS, COLS), full),
            pltpu.VMEM((4 * TAPS, 2 * COLS), full),
            pltpu.VMEM((MEMBERS, 8, COLS), full),
            pltpu.VMEM((MEMBERS, 8, COLS), full),
            pltpu.VMEM((8, COLS), full),
            pltpu.VMEM((RING, 8, COLS), full),
            pltpu.VMEM((8, COLS), full),
            pltpu.SemaphoreType.DMA((7,)),
            pltpu.SemaphoreType.DMA((2,)),
            pltpu.SemaphoreType.DMA((2,)),
            pltpu.SemaphoreType.DMA((2,)),
            pltpu.SemaphoreType.DMA((2,)),
            pltpu.SemaphoreType.DMA((3,)),
            pltpu.SemaphoreType.DMA((3,)),
            pltpu.SemaphoreType.REGULAR((6,)),
        ],
        compiler_params=pltpu.CompilerParams(
            vmem_limit_bytes=VMEM,
            **({"collective_id": 0, "has_side_effects": True} if comm else {}),
        ),
        cost_estimate=pl.CostEstimate(flops=10**10, bytes_accessed=4 * 10**6, transcendentals=10**6),
    )(volume.reshape(shape), taps, offset, upstream.reshape(shape))
    act, gvol, gk, go = pl.pallas_call(
        write_out,
        out_shape=(
            jax.ShapeDtypeStruct(shape, half),
            jax.ShapeDtypeStruct(shape, half),
            jax.ShapeDtypeStruct((27 * CH, CH), full),
            jax.ShapeDtypeStruct((1, CH), full),
        ),
        in_specs=[vmem, vmem, vmem],
        out_specs=(hbm, hbm, hbm, hbm),
        scratch_shapes=[
            pltpu.VMEM((27 * CH, CH), full),
            pltpu.VMEM((1, CH), full),
            pltpu.SemaphoreType.DMA((4,)),
        ],
        compiler_params=pltpu.CompilerParams(vmem_limit_bytes=8 * 1024 * 1024),
        cost_estimate=pl.CostEstimate(flops=10**5, bytes_accessed=3 * 10**6, transcendentals=0),
    )(act, gvol, res)
    return (
        act.reshape(volume.shape),
        gvol.reshape(volume.shape),
        jnp.transpose(gk.reshape(3, 3, 3, CH, CH), (3, 4, 0, 1, 2)),
        go.reshape(CH),
    )


def solution(mesh):
    cells = mesh.shape["batch"] * mesh.shape["slab"] * PLANES * ROWS * COLS
    split = P("batch", None, "slab", None, None)
    return jax.shard_map(
        functools.partial(layer, True, cells**-0.5),
        mesh=mesh,
        in_specs=(split, P(), P(), split),
        out_specs=(split, split, P(), P()),
        check_vma=False,
    )
```
